128 devices in a mesh: group: 16 (over x, y_lo, core), tensor: 8 (over y_hi, z).
Axes of the slice: x: 4, y: 4 (y_hi: 2, y_lo: 2; y = y_hi * 2 + y_lo), z: 4, core: 2. Of those that a mesh axis runs over, the one named last changes fastest.
Arguments:
- tokens: bfloat16 [2, 64, 8192], P(None, 'group'), may hold values from -6 to 6
- queries: bfloat16 [2, 2, 64, 8192], P(None, None, 'group', 'tensor'), may hold values from -40 to 40
- cache_kv: bfloat16 [2, 64, 2048, 2048], P(None, 'group', None, 'tensor'), may hold values from -40 to 40
- old_kv: bfloat16 [2, 8192, 2048], P(None, None, 'tensor'), may hold values from -0.0625 to 0.0625
- new_kv: bfloat16 [2, 8192, 2048], P(None, 'group', 'tensor'), may hold values from -0.0625 to 0.0625
- switch: int32 [2], replicated, may hold values from 0 to 1, each once
- lengths: int32 [64], P('group'), may hold values from 1 to 2048, as said below
Outputs:
- hidden_out: bfloat16 [2, 64, 8192], P(None, 'group', 'tensor')
The draws below stay inside these ranges and needn't reach their ends.
Inputs may be any that keep to these rules, and one draw needn't show every extreme that they name: `switch`: the entries are a permutation of 0 to 1; a layer uses new_kv at every step from its entry on. `lengths`: sequences with an odd index hold 1 to 8 valid positions, sequence 1 exactly 1 and sequence 3 exactly 8; sequences with an even index hold 512 to 2048, sequence 0 exactly 2048.
All inputs are finite; a program needn't handle non-finite values.
Results may differ from the reference program's by a relative error of at most 0.0075.
Values may be sent and summed in bfloat16 or wider, within the bound.
A program may use at most 128 MiB of HBM per device.

```python
import jax
import jax.numpy as jnp
from jax import lax

D = 8192
KVH = 8
QPK = 8
HD = 128
LAYERS = 2
STEPS = 2
CACHE = 2048
SEQS = 64


def draw_cache_kv(key, part):
    key = jax.random.fold_in(key, 11)
    values = jnp.clip(jax.random.normal(key, (LAYERS, SEQS, CACHE, KVH, 2, HD), jnp.float32), -4.0, 4.0)
    return values.reshape(LAYERS, SEQS, CACHE, KVH * 2 * HD).astype(jnp.bfloat16)


def draw_queries(key, part):
    key = jax.random.fold_in(key, 12)
    values = jnp.clip(jax.random.normal(key, (STEPS, LAYERS, SEQS, KVH, QPK, HD), jnp.float32), -4.0, 4.0)
    return values.reshape(STEPS, LAYERS, SEQS, KVH * QPK * HD).astype(jnp.bfloat16)


def draw_lengths(key, part):
    key = jax.random.fold_in(key, 13)
    key_long = jax.random.fold_in(key, 1)
    key_short = jax.random.fold_in(key, 2)
    rows = jnp.arange(SEQS)
    long_len = jax.random.randint(key_long, (SEQS,), CACHE // 4, CACHE + 1)
    short_len = jax.random.randint(key_short, (SEQS,), 1, 9)
    picked = jnp.where(rows % 2 == 1, short_len, long_len)
    picked = jnp.where(rows == 0, CACHE, picked)
    picked = jnp.where(rows == 1, 1, picked)
    picked = jnp.where(rows == 3, 8, picked)
    return picked.astype(jnp.int32)


def block_scale(key, shape, cuts, least, top_value):
    factor_of, own = 1.0, jax.random.fold_in(key, 6)
    for position, shards_of in cuts:
        heights = jnp.exp(jax.random.uniform(jax.random.fold_in(own, position), (shards_of,), jnp.float32, least / len(cuts), top_value / len(cuts)))
        factor_of = factor_of * jnp.repeat(heights, shape[position] // shards_of).reshape([-1 if axis == position else 1 for axis in range(len(shape))])
    return factor_of


def centred(own_key, extent, width, most, pieces=(), kind=jnp.bfloat16):
    values = jax.random.normal(own_key, extent, jnp.float32) * width
    if len(pieces) > 0:
        values = block_scale(own_key, extent, pieces, -0.22, 0.18) * values
    return jnp.clip(values, min=-most, max=most).astype(kind)


def setup_inputs(seed: int = 0) -> dict:
    keys = jax.random.split(jax.random.key(seed), 8)
    tokens = centred(keys[0], (STEPS, SEQS, D), 1.0, 6.0, ((1, 16),))
    queries = draw_queries(jax.random.fold_in(keys[7], 71), 0)
    cache_kv = draw_cache_kv(jax.random.fold_in(keys[7], 71), 0)
    old_kv = centred(keys[3], (LAYERS, D, KVH * 2 * HD), D ** -0.5, 0.0625, ((2, 8),))
    new_kv = centred(keys[4], (LAYERS, D, KVH * 2 * HD), D ** -0.5, 0.0625, ((1, 16), (2, 8)))
    switch = jax.random.permutation(keys[5], LAYERS).astype(jnp.int32)
    lengths = draw_lengths(jax.random.fold_in(keys[7], 71), 0)
    return dict(tokens=tokens, queries=queries, cache_kv=cache_kv, old_kv=old_kv, new_kv=new_kv, switch=switch, lengths=lengths)


def normalize(values):
    return values * lax.rsqrt(lax.optimization_barrier(jnp.mean(values * values, axis=-1, keepdims=True)) + 1e-05)

def attend(query_heads, cache_block, fresh, lengths):
    scale = HD ** (-0.5)

    def per_sequence(item):
        query_one, cache_one, fresh_one, length = item
        query_f = query_one.astype(jnp.float32)
        keys_old = cache_one[:, :, 0].astype(jnp.float32)
        values_old = cache_one[:, :, 1].astype(jnp.float32)
        keys_new = fresh_one[:, :, 0].astype(jnp.float32)
        values_new = fresh_one[:, :, 1].astype(jnp.float32)
        score_old = jnp.einsum('tjid,cjd->tjic', query_f, keys_old) * scale
        valid = jnp.arange(CACHE) < length
        score_old = jnp.where(valid[None, None, None, :], score_old, -1e+30)
        score_new = jnp.einsum('tjid,ujd->tjiu', query_f, keys_new) * scale
        causal = jnp.arange(STEPS)[None, :] <= jnp.arange(STEPS)[:, None]
        score_new = jnp.where(causal[:, None, None, :], score_new, -1e+30)
        top = jnp.maximum(score_old.max(-1, keepdims=True), score_new.max(-1, keepdims=True))
        exp_old = jnp.exp(score_old - top)
        exp_new = jnp.exp(score_new - top)
        total = exp_old.sum(-1, keepdims=True) + exp_new.sum(-1, keepdims=True)
        weight_old = lax.optimization_barrier((exp_old / total).astype(jnp.bfloat16)).astype(jnp.float32)
        weight_new = lax.optimization_barrier((exp_new / total).astype(jnp.bfloat16)).astype(jnp.float32)
        mixed = jnp.einsum('tjic,cjd->tjid', weight_old, values_old) + jnp.einsum('tjiu,ujd->tjid', weight_new, values_new)
        return mixed.astype(jnp.bfloat16)
    result = lax.map(per_sequence, (jnp.swapaxes(query_heads, 0, 1), cache_block, jnp.swapaxes(fresh, 0, 1), lengths))
    return jnp.swapaxes(result, 0, 1).reshape(STEPS, SEQS, D)

def reference(tokens, queries, cache_kv, old_kv, new_kv, switch, lengths):
    hidden = tokens.astype(jnp.float32)
    step_ids = jnp.arange(STEPS)
    for layer in range(LAYERS):
        normed = normalize(hidden).astype(jnp.bfloat16)
        flat_rows = normed.reshape(STEPS * SEQS, D)
        old_proj = jnp.dot(flat_rows, old_kv[layer], preferred_element_type=jnp.float32).reshape(STEPS, SEQS, -1)
        new_proj = jnp.dot(flat_rows, new_kv[layer], preferred_element_type=jnp.float32).reshape(STEPS, SEQS, -1)
        use_new = (step_ids >= switch[layer])[:, None, None]
        fresh = jnp.where(use_new, new_proj, old_proj).astype(jnp.bfloat16).reshape(STEPS, SEQS, KVH, 2, HD)
        query_heads = queries[:, layer].reshape(STEPS, SEQS, KVH, QPK, HD)
        cache_block = cache_kv[layer].reshape(SEQS, CACHE, KVH, 2, HD)
        attended = attend(query_heads, cache_block, fresh, lengths)
        hidden = hidden + attended.astype(jnp.float32)
    return hidden.astype(jnp.bfloat16)
```

```python
import functools
import math

import jax
import jax.numpy as jnp
from jax import lax
from jax.experimental import pallas as pl
from jax.experimental.pallas import tpu as pltpu
from jax.sharding import PartitionSpec as P

MESH = pl.DeviceIdType.MESH
F32, BF16 = jnp.float32, jnp.bfloat16
HD = 128
QPK = 8
LAYERS = 2
STEPS = 2
SEQS = 4
ROWS = STEPS * SEQS
SHORT = 16
FAR = -1e30
UNIT = HD**-0.5 * math.log2(math.e)


def stack_rows(ref_value):
    wide = ref_value.astype(F32)
    return jnp.concatenate([wide[0], wide[1]], axis=0)


def kernel(
    groups,
    tensors,
    tokens,
    queries,
    cache,
    old_kv,
    new_kv,
    switch_hbm,
    lengths_hbm,
    out,
    switch,
    lengths,
    tok_v,
    own_v,
    q_v,
    long_v,
    short_v,
    old_v,
    new_v,
    send_a,
    recv_a,
    send_b,
    recv_b,
    send_c,
    recv_c,
    send_d,
    recv_d,
    load_sem,
    long_sem,
    short_sem,
    send_sem,
    recv_sem,
):
    g = lax.axis_index("group")
    t = lax.axis_index("tensor")
    depth = new_kv.shape[1]
    half = depth // 2
    width = tokens.shape[2]
    block = width // tensors
    home = g // 2

    barrier = pltpu.get_barrier_semaphore()
    for k in range(1, groups):
        pl.semaphore_signal(
            barrier,
            inc=1,
            device_id={"group": lax.rem(g + k, groups), "tensor": t},
            device_id_type=MESH,
        )
    for k in range(1, groups):
        pl.semaphore_signal(
            barrier,
            inc=1,
            device_id={"group": lax.rem(g + k, groups), "tensor": home},
            device_id_type=MESH,
        )

    @pl.when(home != t)
    def _():
        pl.semaphore_signal(
            barrier, inc=1, device_id={"group": g, "tensor": home}, device_id_type=MESH
        )

    loads = [
        pltpu.make_async_copy(tokens, tok_v, load_sem.at[0]),
        pltpu.make_async_copy(
            tokens.at[:, :, pl.ds(pl.multiple_of(t * block, block), block)],
            own_v,
            load_sem.at[1],
        ),
        pltpu.make_async_copy(queries, q_v, load_sem.at[2]),
        pltpu.make_async_copy(new_kv, new_v, load_sem.at[3]),
        pltpu.make_async_copy(
            old_kv.at[:, pl.ds(pl.multiple_of(g * depth, depth), depth), :],
            old_v,
            load_sem.at[4],
        ),
        pltpu.make_async_copy(switch_hbm, switch, load_sem.at[5]),
        pltpu.make_async_copy(lengths_hbm, lengths, load_sem.at[6]),
    ]
    longs = [
        [
            pltpu.make_async_copy(
                cache.at[layer, 2 * j], long_v.at[layer, j], long_sem.at[layer, j]
            )
            for j in range(2)
        ]
        for layer in range(LAYERS)
    ]
    shorts = [
        [
            pltpu.make_async_copy(
                cache.at[layer, 2 * j + 1, pl.ds(0, SHORT)],
                short_v.at[layer, j],
                short_sem.at[layer, j],
            )
            for j in range(2)
        ]
        for layer in range(LAYERS)
    ]
    for copy in loads:
        copy.start()
    for layer in range(LAYERS):
        for j in range(2):
            longs[layer][j].start()
            shorts[layer][j].start()

    loads[0].wait()
    mine = stack_rows(tok_v[...])
    for k in range(groups):
        piece = mine[:, k * depth : (k + 1) * depth]
        send_a[k] = jnp.concatenate([piece[:, :half], piece[:, half:]], axis=0).astype(BF16)
    scale_0 = lax.rsqrt(jnp.sum(mine * mine, axis=1, keepdims=True) / width + 1e-05)

    @pl.when(home != t)
    def _():
        pl.semaphore_wait(barrier, 2 * groups - 1)

    @pl.when(home == t)
    def _():
        pl.semaphore_wait(barrier, 2 * groups - 2)

    def whole(ref, sem):
        return pltpu.make_async_copy(ref, ref, sem)

    def to_group(src, dst, phase, sign, by_slot):
        for k in range(1, groups):
            peer = lax.rem(g + (groups + sign * k), groups)
            pltpu.make_async_remote_copy(
                src_ref=src.at[k if by_slot else peer],
                dst_ref=dst.at[k],
                send_sem=send_sem.at[phase],
                recv_sem=recv_sem.at[phase],
                device_id={"group": peer, "tensor": t},
                device_id_type=MESH,
            ).start()

    to_group(send_a, recv_a, 0, 1, False)
    recv_a[0] = send_a[g]

    row = lax.broadcasted_iota(jnp.int32, (QPK * ROWS, 1), 0)
    row_seq = lax.rem(row, SEQS)

    def stale(layer):
        every = stack_rows(q_v[:, layer])
        q = jnp.concatenate([every[:, i * HD : (i + 1) * HD] for i in range(QPK)], axis=0)
        q16 = q.astype(BF16)
        scores = []
        blocks = []
        for j in range(2):
            longs[layer][j].wait()
            shorts[layer][j].wait()
            for held, seq in ((long_v, 2 * j), (short_v, 2 * j + 1)):
                s = lax.dot_general(
                    q16, held[layer, j, :, :HD], (((1,), (1,)), ((), ())), preferred_element_type=F32
                )
                col = lax.broadcasted_iota(jnp.int32, s.shape, 1)
                keep = (col < lengths[seq]) & (row_seq == seq)
                scores.append(jnp.where(keep, s * UNIT, FAR))
                blocks.append((held, j))
        top = functools.reduce(
            jnp.maximum, [jnp.max(s, axis=1, keepdims=True) for s in scores]
        )
        total = jnp.zeros_like(top)
        mixed = jnp.zeros((QPK * ROWS, HD), F32)
        for s, (held, j) in zip(scores, blocks):
            weight = jnp.exp2(s - top)
            total = total + jnp.sum(weight, axis=1, keepdims=True)
            mixed = mixed + jnp.dot(weight.astype(BF16), held[layer, j, :, HD:], preferred_element_type=F32)
        shape = (QPK, ROWS)
        return (
            q.reshape(*shape, HD),
            top.reshape(*shape, 1),
            total.reshape(*shape, 1),
            mixed.reshape(*shape, HD),
        )

    upper = lax.broadcasted_iota(jnp.int32, (ROWS, HD), 0) < SEQS

    def by_step(fresh):
        other = jnp.concatenate([fresh[SEQS:], fresh[:SEQS]], axis=0)
        return jnp.where(upper, fresh, other), jnp.where(upper, other, fresh)

    def merge(fresh, part):
        q, top, total, mixed = part
        fresh = fresh.astype(BF16).astype(F32)
        key_0, key_1 = by_step(fresh[:, :HD])
        value_0, value_1 = by_step(fresh[:, HD:])
        s_0 = jnp.sum(q * key_0[None], axis=2, keepdims=True) * UNIT
        s_1 = jnp.sum(q * key_1[None], axis=2, keepdims=True) * UNIT
        s_1 = jnp.where(upper[None, :, :1], FAR, s_1)
        peak = jnp.maximum(top, jnp.maximum(s_0, s_1))
        keep = jnp.exp2(top - peak)
        w_0 = jnp.exp2(s_0 - peak)
        w_1 = jnp.exp2(s_1 - peak)
        norm = 1.0 / (total * keep + w_0 + w_1)
        result = (mixed * keep + w_0 * value_0[None] + w_1 * value_1[None]) * norm
        return result.astype(BF16).astype(F32)

    def project(layer, features):
        flat = jnp.concatenate(
            [features[:, :ROWS].reshape(-1, half), features[:, ROWS:].reshape(-1, half)], axis=1
        ).astype(BF16)
        by_new = jnp.dot(flat, new_v[layer], preferred_element_type=F32)
        by_old = jnp.dot(flat, old_v[layer], preferred_element_type=F32)
        step = lax.rem(lax.broadcasted_iota(jnp.int32, by_new.shape, 0), ROWS) // SEQS
        picked = jnp.where(step >= switch[layer], by_new, by_old)
        return picked.reshape(groups, ROWS, -1)

    for copy in loads[1:]:
        copy.wait()
    part_0 = stale(0)

    rest = pl.ds(1, groups - 1)
    whole(recv_a.at[rest], recv_sem.at[0]).wait()
    products = project(0, recv_a[...].astype(F32))
    send_b[...] = products
    to_group(send_b, recv_b, 1, -1, True)
    recv_b[0] = products[0]
    part_1 = stale(1)

    whole(recv_b.at[rest], recv_sem.at[1]).wait()
    attended_0 = merge(jnp.sum(recv_b[...], axis=0) * scale_0, part_0)
    pair = QPK // 4
    for h in range(2):
        send_c[h] = jnp.concatenate(
            [
                jnp.concatenate([attended_0[4 * h + 2 * r + c] for c in range(pair)], axis=1)
                for r in range(2)
            ],
            axis=0,
        ).astype(BF16)

    for h in range(2):
        target = 2 * t + h
        slot = lax.rem(target + groups - g, groups)

        def copy_c(j):
            return pltpu.make_async_remote_copy(
                src_ref=send_c.at[h],
                dst_ref=recv_c.at[slot],
                send_sem=send_sem.at[2],
                recv_sem=recv_sem.at[2],
                device_id={"group": target, "tensor": lax.rem(t + j, tensors)},
                device_id_type=MESH,
            )

        for j in range(1, tensors):
            copy_c(j).start()

        @pl.when(target != g)
        def _():
            copy_c(0).start()

        @pl.when(target == g)
        def _():
            pltpu.make_async_copy(send_c.at[h], recv_c.at[slot], recv_sem.at[2]).start()

    whole(recv_c, recv_sem.at[2]).wait()
    hidden = recv_a[...].astype(F32) + recv_c[...].astype(F32)
    square = jnp.sum(hidden * hidden, axis=2, keepdims=True)
    square = square[:, :ROWS] + square[:, ROWS:]
    products = project(1, hidden)
    products = jnp.concatenate(
        [products, jnp.broadcast_to(square, (groups, ROWS, HD))], axis=2
    )
    send_d[...] = products
    to_group(send_d, recv_d, 3, -1, True)
    recv_d[0] = products[0]
    own = stack_rows(own_v[...])

    whole(recv_d.at[rest], recv_sem.at[3]).wait()
    summed = jnp.sum(recv_d[...], axis=0)
    scale_1 = lax.rsqrt(summed[:, 2 * HD : 2 * HD + 1] / width + 1e-05)
    attended_1 = merge(summed[:, : 2 * HD] * scale_1, part_1)
    for i in range(QPK):
        at = slice(i * HD, (i + 1) * HD)
        out[:, at] = own[:, at] + attended_0[i] + attended_1[i]

    for phase, src in ((0, send_a), (1, send_b), (3, send_d)):
        whole(src.at[rest], send_sem.at[phase]).wait()

    @pl.when(home != t)
    def _():
        whole(recv_c, send_sem.at[2]).wait()

    @pl.when(home == t)
    def _():
        whole(recv_c.at[rest], send_sem.at[2]).wait()


def solution(mesh):
    groups, tensors = mesh.shape["group"], mesh.shape["tensor"]

    def per_device(tokens, queries, cache_kv, old_kv, new_kv, switch, lengths):
        depth = new_kv.shape[1]
        half = depth // 2
        block = tokens.shape[2] // tensors
        cache_len = cache_kv.shape[2]
        hbm = pl.BlockSpec(memory_space=pltpu.HBM)
        vmem = pltpu.VMEM
        result = pl.pallas_call(
            functools.partial(kernel, groups, tensors),
            out_shape=jax.ShapeDtypeStruct((ROWS, block), F32),
            in_specs=[hbm] * 7,
            out_specs=pl.BlockSpec(memory_space=vmem),
            scratch_shapes=[
                pltpu.SMEM(switch.shape, jnp.int32),
                pltpu.SMEM(lengths.shape, jnp.int32),
                vmem(tokens.shape, BF16),
                vmem((STEPS, SEQS, block), BF16),
                vmem(queries.shape, BF16),
                vmem((LAYERS, 2, cache_len, 2 * HD), BF16),
                vmem((LAYERS, 2, SHORT, 2 * HD), BF16),
                vmem(new_kv.shape, BF16),
                vmem(new_kv.shape, BF16),
                vmem((groups, 2 * ROWS, half), BF16),
                vmem((groups, 2 * ROWS, half), BF16),
                vmem((groups, ROWS, 2 * HD), F32),
                vmem((groups, ROWS, 2 * HD), F32),
                vmem((2, 2 * ROWS, half), BF16),
                vmem((groups, 2 * ROWS, half), BF16),
                vmem((groups, ROWS, 3 * HD), F32),
                vmem((groups, ROWS, 3 * HD), F32),
                pltpu.SemaphoreType.DMA((7,)),
                pltpu.SemaphoreType.DMA((LAYERS, 2)),
                pltpu.SemaphoreType.DMA((LAYERS, 2)),
                pltpu.SemaphoreType.DMA((4,)),
                pltpu.SemaphoreType.DMA((4,)),
            ],
            compiler_params=pltpu.CompilerParams(
                collective_id=0, has_side_effects=True, vmem_limit_bytes=40 * 2**20
            ),
        )(tokens, queries, cache_kv, old_kv, new_kv, switch, lengths)
        return result.astype(BF16).reshape(STEPS, SEQS, block)

    return jax.shard_map(
        per_device,
        mesh=mesh,
        in_specs=(
            P(None, "group", None),
            P(None, None, "group", "tensor"),
            P(None, "group", None, "tensor"),
            P(None, None, "tensor"),
            P(None, "group", "tensor"),
            P(),
            P("group"),
        ),
        out_specs=P(None, "group", "tensor"),
        check_vma=False,
    )
```

```python
import functools
import math

import jax
import jax.numpy as jnp
from jax import lax
from jax.experimental import pallas as pl
from jax.experimental.pallas import tpu as pltpu
from jax.sharding import PartitionSpec as P

MESH = pl.DeviceIdType.MESH
F32, BF16 = jnp.float32, jnp.bfloat16
HD = 128
QPK = 8
LAYERS = 2
STEPS = 2
SEQS = 4
ROWS = STEPS * SEQS
SHORT = 16
FAR = -1e30
UNIT = HD**-0.5 * math.log2(math.e)


def stack_rows(ref_value):
    wide = ref_value.astype(F32)
    return jnp.concatenate([wide[0], wide[1]], axis=0)


def kernel(
    groups,
    tensors,
    tokens,
    queries,
    cache,
    old_kv,
    new_kv,
    switch_hbm,
    lengths_hbm,
    out,
    switch,
    lengths,
    tok_v,
    own_v,
    q_v,
    long_v,
    short_v,
    old_0,
    old_1,
    new_0,
    new_1,
    send_a,
    recv_a,
    send_b,
    recv_b,
    send_c,
    recv_c,
    recv_t,
    send_d,
    recv_d,
    load_sem,
    long_sem,
    short_sem,
    send_sem,
    recv_sem,
):
    g = lax.axis_index("group")
    t = lax.axis_index("tensor")
    depth = new_kv.shape[1]
    half = depth // 2
    width = tokens.shape[2]
    block = width // tensors
    x, y, core = g // 4, lax.rem(g // 2, 2), lax.rem(g, 2)

    def device(group, tensor):
        return {"group": group, "tensor": tensor}

    def holder(row_block, column_block):
        across = lax.rem(row_block // 4 + column_block // 2, 4)
        along = lax.rem(row_block // 2 + column_block, 2)
        return 4 * across + 2 * along + lax.rem(row_block, 2)

    there = device(holder(g, t), g // 2)
    column = 2 * lax.rem(x + 4 - t // 2, 4) + lax.rem(y + t, 2)
    origin = device(2 * t + core, column)

    def same(other):
        return (other["group"] == g) & (other["tensor"] == t)

    barrier = pltpu.get_barrier_semaphore()

    def greet(other):
        pl.semaphore_signal(barrier, inc=1, device_id=other, device_id_type=MESH)

    def greet_other(other):
        @pl.when(jnp.logical_not(same(other)))
        def _():
            greet(other)

    for k in range(1, groups):
        greet(device(lax.rem(g + k, groups), t))
    for k in range(1, tensors):
        greet(device(g, lax.rem(t + k, tensors)))
    greet_other(origin)
    for block_index in range(groups):
        greet_other(device(holder(block_index, t), block_index // 2))

    loads = [
        pltpu.make_async_copy(tokens, tok_v, load_sem.at[0]),
        pltpu.make_async_copy(
            tokens.at[:, :, pl.ds(pl.multiple_of(t * block, block), block)],
            own_v,
            load_sem.at[1],
        ),
        pltpu.make_async_copy(queries, q_v, load_sem.at[2]),
        pltpu.make_async_copy(new_kv.at[0], new_0, load_sem.at[3]),
        pltpu.make_async_copy(
            old_kv.at[0, pl.ds(pl.multiple_of(g * depth, depth), depth), :],
            old_0,
            load_sem.at[4],
        ),
        pltpu.make_async_copy(switch_hbm, switch, load_sem.at[5]),
        pltpu.make_async_copy(lengths_hbm, lengths, load_sem.at[6]),
    ]
    late = pltpu.make_async_copy(old_kv.at[1], old_1, load_sem.at[7])
    longs = [
        [
            pltpu.make_async_copy(
                cache.at[layer, 2 * j], long_v.at[layer, j], long_sem.at[layer, j]
            )
            for j in range(2)
        ]
        for layer in range(LAYERS)
    ]
    shorts = [
        [
            pltpu.make_async_copy(
                cache.at[layer, 2 * j + 1, pl.ds(0, SHORT)],
                short_v.at[layer, j],
                short_sem.at[layer, j],
            )
            for j in range(2)
        ]
        for layer in range(LAYERS)
    ]
    for copy in loads:
        copy.start()
    for layer in range(LAYERS):
        for j in range(2):
            longs[layer][j].start()
            shorts[layer][j].start()
    late.start()

    loads[0].wait()
    mine = stack_rows(tok_v[...])
    for k in range(groups):
        piece = mine[:, k * depth : (k + 1) * depth]
        send_a[k] = jnp.concatenate([piece[:, :half], piece[:, half:]], axis=0).astype(BF16)
    scale_0 = lax.rsqrt(jnp.sum(mine * mine, axis=1, keepdims=True) / width + 1e-05)

    waited = groups - 1 + tensors - 1 + 1 + groups
    stays = same(there).astype(jnp.int32) + (column == t).astype(jnp.int32)
    pl.semaphore_wait(barrier, waited - stays)

    def whole(ref, sem):
        return pltpu.make_async_copy(ref, ref, sem)

    def to_group(src, dst, phase, sign, by_slot):
        for k in range(1, groups):
            peer = lax.rem(g + (groups + sign * k), groups)
            pltpu.make_async_remote_copy(
                src_ref=src.at[k if by_slot else peer],
                dst_ref=dst.at[k],
                send_sem=send_sem.at[phase],
                recv_sem=recv_sem.at[phase],
                device_id={"group": peer, "tensor": t},
                device_id_type=MESH,
            ).start()

    to_group(send_a, recv_a, 0, 1, False)
    recv_a[0] = send_a[g]

    def put(src, dst, other, phase):
        @pl.when(jnp.logical_not(same(other)))
        def _():
            pltpu.make_async_remote_copy(
                src_ref=src,
                dst_ref=dst,
                send_sem=send_sem.at[phase],
                recv_sem=recv_sem.at[phase],
                device_id=other,
                device_id_type=MESH,
            ).start()

        @pl.when(same(other))
        def _():
            pltpu.make_async_copy(src, dst, recv_sem.at[phase]).start()

    put(new_kv.at[1], new_1, there, 4)

    row = lax.broadcasted_iota(jnp.int32, (QPK * ROWS, 1), 0)
    row_seq = lax.rem(row, SEQS)

    def stale(layer):
        every = stack_rows(q_v[:, layer])
        q = jnp.concatenate([every[:, i * HD : (i + 1) * HD] for i in range(QPK)], axis=0)
        q16 = q.astype(BF16)
        scores = []
        blocks = []
        for j in range(2):
            longs[layer][j].wait()
            shorts[layer][j].wait()
            for held, seq in ((long_v, 2 * j), (short_v, 2 * j + 1)):
                s = lax.dot_general(
                    q16, held[layer, j, :, :HD], (((1,), (1,)), ((), ())), preferred_element_type=F32
                )
                col = lax.broadcasted_iota(jnp.int32, s.shape, 1)
                keep = (col < lengths[seq]) & (row_seq == seq)
                scores.append(jnp.where(keep, s * UNIT, FAR))
                blocks.append((held, j))
        top = functools.reduce(
            jnp.maximum, [jnp.max(s, axis=1, keepdims=True) for s in scores]
        )
        total = jnp.zeros_like(top)
        mixed = jnp.zeros((QPK * ROWS, HD), F32)
        for s, (held, j) in zip(scores, blocks):
            weight = jnp.exp2(s - top)
            total = total + jnp.sum(weight, axis=1, keepdims=True)
            mixed = mixed + jnp.dot(weight.astype(BF16), held[layer, j, :, HD:], preferred_element_type=F32)
        shape = (QPK, ROWS)
        return (
            q.reshape(*shape, HD),
            top.reshape(*shape, 1),
            total.reshape(*shape, 1),
            mixed.reshape(*shape, HD),
        )

    upper = lax.broadcasted_iota(jnp.int32, (ROWS, HD), 0) < SEQS

    def by_step(fresh):
        other = jnp.concatenate([fresh[SEQS:], fresh[:SEQS]], axis=0)
        return jnp.where(upper, fresh, other), jnp.where(upper, other, fresh)

    def merge(fresh, part):
        q, top, total, mixed = part
        fresh = fresh.astype(BF16).astype(F32)
        key_0, key_1 = by_step(fresh[:, :HD])
        value_0, value_1 = by_step(fresh[:, HD:])
        s_0 = jnp.sum(q * key_0[None], axis=2, keepdims=True) * UNIT
        s_1 = jnp.sum(q * key_1[None], axis=2, keepdims=True) * UNIT
        s_1 = jnp.where(upper[None, :, :1], FAR, s_1)
        peak = jnp.maximum(top, jnp.maximum(s_0, s_1))
        keep = jnp.exp2(top - peak)
        w_0 = jnp.exp2(s_0 - peak)
        w_1 = jnp.exp2(s_1 - peak)
        norm = 1.0 / (total * keep + w_0 + w_1)
        result = (mixed * keep + w_0 * value_0[None] + w_1 * value_1[None]) * norm
        return result.astype(BF16).astype(F32)

    def flatten(features):
        return jnp.concatenate(
            [features[:, :ROWS].reshape(-1, half), features[:, ROWS:].reshape(-1, half)], axis=1
        ).astype(BF16)

    for copy in loads[1:]:
        copy.wait()
    part_0 = stale(0)

    rest = pl.ds(1, groups - 1)
    whole(recv_a.at[rest], recv_sem.at[0]).wait()
    flat = flatten(recv_a[...].astype(F32))
    by_new = jnp.dot(flat, new_0[...], preferred_element_type=F32)
    by_old = jnp.dot(flat, old_0[...], preferred_element_type=F32)
    step = lax.rem(lax.broadcasted_iota(jnp.int32, by_new.shape, 0), ROWS) // SEQS
    products = jnp.where(step >= switch[0], by_new, by_old).reshape(groups, ROWS, -1)
    send_b[...] = products
    to_group(send_b, recv_b, 1, -1, True)
    recv_b[0] = products[0]
    part_1 = stale(1)

    whole(recv_b.at[rest], recv_sem.at[1]).wait()
    attended_0 = merge(jnp.sum(recv_b[...], axis=0) * scale_0, part_0)
    own = stack_rows(own_v[...])
    hidden = [own[:, i * HD : (i + 1) * HD] + attended_0[i] for i in range(QPK)]
    for h in range(2):
        send_c[h] = jnp.concatenate(
            [jnp.concatenate(hidden[4 * h + 2 * r : 4 * h + 2 * r + 2], axis=1) for r in range(2)],
            axis=0,
        ).astype(BF16)

    for k in range(1, groups):
        peer = lax.rem(g + k, groups)
        pltpu.make_async_remote_copy(
            src_ref=send_c.at[lax.rem(peer, 2)],
            dst_ref=recv_c.at[g],
            send_sem=send_sem.at[2],
            recv_sem=recv_sem.at[2],
            device_id=device(peer, t),
            device_id_type=MESH,
        ).start()
    pltpu.make_async_copy(send_c.at[core], recv_c.at[g], recv_sem.at[2]).start()
    for k in range(1, tensors):
        pltpu.make_async_remote_copy(
            src_ref=send_c,
            dst_ref=recv_t.at[t],
            send_sem=send_sem.at[5],
            recv_sem=recv_sem.at[5],
            device_id=device(g, lax.rem(t + k, tensors)),
            device_id_type=MESH,
        ).start()
    pltpu.make_async_copy(send_c, recv_t.at[t], recv_sem.at[5]).start()

    whole(new_1, recv_sem.at[4]).wait()
    whole(recv_c, recv_sem.at[2]).wait()
    flat = flatten(recv_c[...].astype(F32))
    send_d[...] = jnp.dot(flat, new_1[...], preferred_element_type=F32).reshape(groups, ROWS, -1)
    for k in range(groups):
        peer = lax.rem(g + k, groups)
        put(send_d.at[peer], recv_d.at[2 * t + core], device(peer, column), 3)

    late.wait()
    whole(recv_t, recv_sem.at[5]).wait()
    parts = [recv_t[i, h].astype(F32) for i in range(tensors) for h in range(2)]
    wide = jnp.concatenate([part[at : at + ROWS] for part in parts for at in (0, ROWS)], axis=1)
    scale_1 = lax.rsqrt(jnp.sum(wide * wide, axis=1, keepdims=True) / width + 1e-05)
    by_old = jnp.dot(wide.astype(BF16), old_1[...], preferred_element_type=F32)
    row_step = lax.broadcasted_iota(jnp.int32, by_old.shape, 0) // SEQS

    whole(recv_d, recv_sem.at[3]).wait()
    summed = jnp.where(row_step >= switch[1], jnp.sum(recv_d[...], axis=0), by_old)
    attended_1 = merge(summed * scale_1, part_1)
    for i in range(QPK):
        out[:, i * HD : (i + 1) * HD] = hidden[i] + attended_1[i]

    for phase, src in ((0, send_a), (1, send_b), (2, recv_c)):
        whole(src.at[rest], send_sem.at[phase]).wait()
    whole(recv_t.at[pl.ds(1, tensors - 1)], send_sem.at[5]).wait()

    @pl.when(jnp.logical_not(same(there)))
    def _():
        whole(new_1, send_sem.at[4]).wait()

    @pl.when(column != t)
    def _():
        whole(send_d, send_sem.at[3]).wait()

    @pl.when(column == t)
    def _():
        whole(send_d.at[rest], send_sem.at[3]).wait()


def solution(mesh):
    groups, tensors = mesh.shape["group"], mesh.shape["tensor"]

    def per_device(tokens, queries, cache_kv, old_kv, new_kv, switch, lengths):
        depth = new_kv.shape[1]
        half = depth // 2
        block = tokens.shape[2] // tensors
        cache_len = cache_kv.shape[2]
        hbm = pl.BlockSpec(memory_space=pltpu.HBM)
        vmem = pltpu.VMEM
        result = pl.pallas_call(
            functools.partial(kernel, groups, tensors),
            out_shape=jax.ShapeDtypeStruct((ROWS, block), F32),
            in_specs=[hbm] * 7,
            out_specs=pl.BlockSpec(memory_space=vmem),
            scratch_shapes=[
                pltpu.SMEM(switch.shape, jnp.int32),
                pltpu.SMEM(lengths.shape, jnp.int32),
                vmem(tokens.shape, BF16),
                vmem((STEPS, SEQS, block), BF16),
                vmem(queries.shape, BF16),
                vmem((LAYERS, 2, cache_len, 2 * HD), BF16),
                vmem((LAYERS, 2, SHORT, 2 * HD), BF16),
                vmem((depth, 2 * HD), BF16),
                vmem(old_kv.shape[1:], BF16),
                vmem((depth, 2 * HD), BF16),
                vmem((depth, 2 * HD), BF16),
                vmem((groups, 2 * ROWS, half), BF16),
                vmem((groups, 2 * ROWS, half), BF16),
                vmem((groups, ROWS, 2 * HD), F32),
                vmem((groups, ROWS, 2 * HD), F32),
                vmem((2, 2 * ROWS, half), BF16),
                vmem((groups, 2 * ROWS, half), BF16),
                vmem((tensors, 2, 2 * ROWS, half), BF16),
                vmem((groups, ROWS, 2 * HD), F32),
                vmem((groups, ROWS, 2 * HD), F32),
                pltpu.SemaphoreType.DMA((8,)),
                pltpu.SemaphoreType.DMA((LAYERS, 2)),
                pltpu.SemaphoreType.DMA((LAYERS, 2)),
                pltpu.SemaphoreType.DMA((6,)),
                pltpu.SemaphoreType.DMA((6,)),
            ],
            compiler_params=pltpu.CompilerParams(
                collective_id=0, has_side_effects=True, vmem_limit_bytes=56 * 2**20
            ),
        )(tokens, queries, cache_kv, old_kv, new_kv, switch, lengths)
        return result.astype(BF16).reshape(STEPS, SEQS, block)

    return jax.shard_map(
        per_device,
        mesh=mesh,
        in_specs=(
            P(None, "group", None),
            P(None, None, "group", "tensor"),
            P(None, "group", None, "tensor"),
            P(None, None, "tensor"),
            P(None, "group", "tensor"),
            P(),
            P("group"),
        ),
        out_specs=P(None, "group", "tensor"),
        check_vma=False,
    )
```

```python
import functools
import math

import jax
import jax.numpy as jnp
from jax import lax
from jax.experimental import pallas as pl
from jax.experimental.pallas import tpu as pltpu
from jax.sharding import PartitionSpec as P

MESH = pl.DeviceIdType.MESH
F32, BF16 = jnp.float32, jnp.bfloat16
HD = 128
QPK = 8
LAYERS = 2
STEPS = 2
SEQS = 4
ROWS = STEPS * SEQS
SHORT = 16
FAR = -1e30
UNIT = HD**-0.5 * math.log2(math.e)


def stack_rows(ref_value):
    wide = ref_value.astype(F32)
    return jnp.concatenate([wide[0], wide[1]], axis=0)


def kernel(
    groups,
    tensors,
    tokens,
    queries,
    cache,
    old_kv,
    new_kv,
    switch_hbm,
    lengths_hbm,
    out,
    switch,
    lengths,
    tok_v,
    own_v,
    q_v,
    long_v,
    short_v,
    old_0,
    old_1,
    new_0,
    new_1,
    send_a,
    recv_a,
    send_b,
    recv_b,
    send_c,
    recv_c,
    recv_t,
    send_d,
    recv_d,
    load_sem,
    long_sem,
    short_sem,
    send_sem,
    recv_sem,
    near_sem,
    far_sem,
):
    g = lax.axis_index("group")
    t = lax.axis_index("tensor")
    depth = new_kv.shape[1]
    half = depth // 2
    width = tokens.shape[2]
    block = width // tensors
    x, y, core = g // 4, lax.rem(g // 2, 2), lax.rem(g, 2)

    def device(group, tensor):
        return {"group": group, "tensor": tensor}

    def holder(row_block, column_block):
        side = lax.rem(row_block, 2)
        across = lax.rem(row_block // 4 + column_block // 2 + 2 * side, 4)
        along = lax.rem(row_block // 2 + column_block + side, 2)
        return 4 * across + 2 * along + side

    def route(side):
        goes = device(holder(2 * (g // 2) + side, t), g // 2)
        return goes, 2 * lax.rem(x + 8 - t // 2 - 2 * side, 4) + lax.rem(y + t + side, 2)

    def targets(side):
        goes, columns = route(side)
        yield goes
        for group in range(groups):
            yield device(group, columns)

    there, column = route(core)
    origin = device(2 * t + core, column)

    def same(other):
        return (other["group"] == g) & (other["tensor"] == t)

    barrier = pltpu.get_barrier_semaphore()
    mate = device(g + 1 - 2 * core, t)

    def greet(other):
        pl.semaphore_signal(barrier, inc=1, device_id=other, device_id_type=MESH)

    def same_chip(other):
        return (other["group"] // 2 == g // 2) & (other["tensor"] == t)

    def senders():
        yield origin
        for block_index in range(groups):
            yield device(holder(block_index, t), block_index // 2)

    for k in range(1, groups // 2):
        greet(device(2 * lax.rem(g // 2 + k, groups // 2), t))

    @pl.when(core == 1)
    def _():
        greet(mate)

    for k in range(1, tensors):
        greet(device(g - core + 1, lax.rem(t + k, tensors)))
    for other in senders():

        @pl.when(jnp.logical_not(same_chip(other)))
        def _():
            greet(device(2 * (other["group"] // 2) + 1, other["tensor"]))

    loads = [
        pltpu.make_async_copy(tokens, tok_v, load_sem.at[0]),
        pltpu.make_async_copy(
            tokens.at[:, :, pl.ds(pl.multiple_of(t * block, block), block)],
            own_v,
            load_sem.at[1],
        ),
        pltpu.make_async_copy(queries, q_v, load_sem.at[2]),
        pltpu.make_async_copy(new_kv.at[0], new_0, load_sem.at[3]),
        pltpu.make_async_copy(
            old_kv.at[0, pl.ds(pl.multiple_of(g * depth, depth), depth), :],
            old_0,
            load_sem.at[4],
        ),
        pltpu.make_async_copy(switch_hbm, switch, load_sem.at[5]),
        pltpu.make_async_copy(lengths_hbm, lengths, load_sem.at[6]),
    ]
    late = pltpu.make_async_copy(old_kv.at[1], old_1, load_sem.at[7])
    longs = [
        [
            pltpu.make_async_copy(
                cache.at[layer, 2 * j], long_v.at[layer, j], long_sem.at[layer, j]
            )
            for j in range(2)
        ]
        for layer in range(LAYERS)
    ]
    shorts = [
        [
            pltpu.make_async_copy(
                cache.at[layer, 2 * j + 1, pl.ds(0, SHORT)],
                short_v.at[layer, j],
                short_sem.at[layer, j],
            )
            for j in range(2)
        ]
        for layer in range(LAYERS)
    ]
    for copy in loads:
        copy.start()
    for layer in range(LAYERS):
        for j in range(2):
            longs[layer][j].start()
            shorts[layer][j].start()
    late.start()

    loads[0].wait()
    mine = stack_rows(tok_v[...])
    for k in range(groups):
        piece = mine[:, k * depth : (k + 1) * depth]
        send_a[k] = jnp.concatenate([piece[:, :half], piece[:, half:]], axis=0).astype(BF16)
    scale_0 = lax.rsqrt(jnp.sum(mine * mine, axis=1, keepdims=True) / width + 1e-05)

    @pl.when(core == 0)
    def _():
        pl.semaphore_wait(barrier, groups - 1)
        pl.semaphore_signal(near_sem, inc=1, device_id=mate, device_id_type=MESH)

    @pl.when(core == 1)
    def _():
        pl.semaphore_wait(near_sem, 1)

    def far_barrier():
        count = 2 * (tensors - 1)
        for other_core in range(2):
            for other in targets(other_core):
                count = count + jnp.logical_not(same_chip(other)).astype(jnp.int32)

        @pl.when(core == 1)
        def _():
            pl.semaphore_wait(barrier, count)
            pl.semaphore_signal(far_sem, inc=1, device_id=mate, device_id_type=MESH)

        @pl.when(core == 0)
        def _():
            pl.semaphore_wait(far_sem, 1)

    def whole(ref, sem):
        return pltpu.make_async_copy(ref, ref, sem)

    def to_group(src, dst, phase, sign, by_slot):
        for k in range(1, groups):
            peer = lax.rem(g + (groups + sign * k), groups)
            pltpu.make_async_remote_copy(
                src_ref=src.at[k if by_slot else peer],
                dst_ref=dst.at[k],
                send_sem=send_sem.at[phase],
                recv_sem=recv_sem.at[phase],
                device_id={"group": peer, "tensor": t},
                device_id_type=MESH,
            ).start()

    to_group(send_a, recv_a, 0, 1, False)
    recv_a[0] = send_a[g]

    def put(src, dst, other, phase):
        @pl.when(jnp.logical_not(same(other)))
        def _():
            pltpu.make_async_remote_copy(
                src_ref=src,
                dst_ref=dst,
                send_sem=send_sem.at[phase],
                recv_sem=recv_sem.at[phase],
                device_id=other,
                device_id_type=MESH,
            ).start()

        @pl.when(same(other))
        def _():
            pltpu.make_async_copy(src, dst, recv_sem.at[phase]).start()

    far_barrier()
    put(new_kv.at[1], new_1, there, 4)

    row = lax.broadcasted_iota(jnp.int32, (QPK * ROWS, 1), 0)
    row_seq = lax.rem(row, SEQS)

    def stale(layer):
        every = stack_rows(q_v[:, layer])
        q = jnp.concatenate([every[:, i * HD : (i + 1) * HD] for i in range(QPK)], axis=0)
        q16 = q.astype(BF16)
        scores = []
        blocks = []
        for j in range(2):
            longs[layer][j].wait()
            shorts[layer][j].wait()
            for held, seq in ((long_v, 2 * j), (short_v, 2 * j + 1)):
                s = lax.dot_general(
                    q16, held[layer, j, :, :HD], (((1,), (1,)), ((), ())), preferred_element_type=F32
                )
                col = lax.broadcasted_iota(jnp.int32, s.shape, 1)
                keep = (col < lengths[seq]) & (row_seq == seq)
                scores.append(jnp.where(keep, s * UNIT, FAR))
                blocks.append((held, j))
        top = functools.reduce(
            jnp.maximum, [jnp.max(s, axis=1, keepdims=True) for s in scores]
        )
        total = jnp.zeros_like(top)
        mixed = jnp.zeros((QPK * ROWS, HD), F32)
        for s, (held, j) in zip(scores, blocks):
            weight = jnp.exp2(s - top)
            total = total + jnp.sum(weight, axis=1, keepdims=True)
            mixed = mixed + jnp.dot(weight.astype(BF16), held[layer, j, :, HD:], preferred_element_type=F32)
        shape = (QPK, ROWS)
        return (
            q.reshape(*shape, HD),
            top.reshape(*shape, 1),
            total.reshape(*shape, 1),
            mixed.reshape(*shape, HD),
        )

    upper = lax.broadcasted_iota(jnp.int32, (ROWS, HD), 0) < SEQS

    def by_step(fresh):
        other = jnp.concatenate([fresh[SEQS:], fresh[:SEQS]], axis=0)
        return jnp.where(upper, fresh, other), jnp.where(upper, other, fresh)

    def merge(fresh, part):
        q, top, total, mixed = part
        fresh = fresh.astype(BF16).astype(F32)
        key_0, key_1 = by_step(fresh[:, :HD])
        value_0, value_1 = by_step(fresh[:, HD:])
        s_0 = jnp.sum(q * key_0[None], axis=2, keepdims=True) * UNIT
        s_1 = jnp.sum(q * key_1[None], axis=2, keepdims=True) * UNIT
        s_1 = jnp.where(upper[None, :, :1], FAR, s_1)
        peak = jnp.maximum(top, jnp.maximum(s_0, s_1))
        keep = jnp.exp2(top - peak)
        w_0 = jnp.exp2(s_0 - peak)
        w_1 = jnp.exp2(s_1 - peak)
        norm = 1.0 / (total * keep + w_0 + w_1)
        result = (mixed * keep + w_0 * value_0[None] + w_1 * value_1[None]) * norm
        return result.astype(BF16).astype(F32)

    def flatten(features):
        return jnp.concatenate(
            [features[:, :ROWS].reshape(-1, half), features[:, ROWS:].reshape(-1, half)], axis=1
        ).astype(BF16)

    for copy in loads[1:]:
        copy.wait()
    part_0 = stale(0)

    rest = pl.ds(1, groups - 1)
    whole(recv_a.at[rest], recv_sem.at[0]).wait()
    flat = flatten(recv_a[...].astype(F32))
    by_new = jnp.dot(flat, new_0[...], preferred_element_type=F32)
    by_old = jnp.dot(flat, old_0[...], preferred_element_type=F32)
    step = lax.rem(lax.broadcasted_iota(jnp.int32, by_new.shape, 0), ROWS) // SEQS
    products = jnp.where(step >= switch[0], by_new, by_old).reshape(groups, ROWS, -1)
    send_b[...] = products
    to_group(send_b, recv_b, 1, -1, True)
    recv_b[0] = products[0]
    part_1 = stale(1)

    whole(recv_b.at[rest], recv_sem.at[1]).wait()
    attended_0 = merge(jnp.sum(recv_b[...], axis=0) * scale_0, part_0)
    own = stack_rows(own_v[...])
    hidden = [own[:, i * HD : (i + 1) * HD] + attended_0[i] for i in range(QPK)]
    for h in range(2):
        send_c[h] = jnp.concatenate(
            [jnp.concatenate(hidden[4 * h + 2 * r : 4 * h + 2 * r + 2], axis=1) for r in range(2)],
            axis=0,
        ).astype(BF16)

    for k in range(1, groups):
        peer = lax.rem(g + k, groups)
        pltpu.make_async_remote_copy(
            src_ref=send_c.at[lax.rem(peer, 2)],
            dst_ref=recv_c.at[g],
            send_sem=send_sem.at[2],
            recv_sem=recv_sem.at[2],
            device_id=device(peer, t),
            device_id_type=MESH,
        ).start()
    pltpu.make_async_copy(send_c.at[core], recv_c.at[g], recv_sem.at[2]).start()
    for k in range(1, tensors):
        pltpu.make_async_remote_copy(
            src_ref=send_c,
            dst_ref=recv_t.at[t],
            send_sem=send_sem.at[5],
            recv_sem=recv_sem.at[5],
            device_id=device(g, lax.rem(t + k, tensors)),
            device_id_type=MESH,
        ).start()
    pltpu.make_async_copy(send_c, recv_t.at[t], recv_sem.at[5]).start()

    whole(new_1, recv_sem.at[4]).wait()
    whole(recv_c, recv_sem.at[2]).wait()
    flat = flatten(recv_c[...].astype(F32))
    send_d[...] = jnp.dot(flat, new_1[...], preferred_element_type=F32).reshape(groups, ROWS, -1)
    for k in range(groups):
        peer = lax.rem(g + k, groups)
        put(send_d.at[peer], recv_d.at[2 * t + core], device(peer, column), 3)

    late.wait()
    whole(recv_t, recv_sem.at[5]).wait()
    parts = [recv_t[i, h].astype(F32) for i in range(tensors) for h in range(2)]
    wide = jnp.concatenate([part[at : at + ROWS] for part in parts for at in (0, ROWS)], axis=1)
    scale_1 = lax.rsqrt(jnp.sum(wide * wide, axis=1, keepdims=True) / width + 1e-05)
    by_old = jnp.dot(wide.astype(BF16), old_1[...], preferred_element_type=F32)
    row_step = lax.broadcasted_iota(jnp.int32, by_old.shape, 0) // SEQS

    whole(recv_d, recv_sem.at[3]).wait()
    summed = jnp.where(row_step >= switch[1], jnp.sum(recv_d[...], axis=0), by_old)
    attended_1 = merge(summed * scale_1, part_1)
    for i in range(QPK):
        rows = (hidden[i] + attended_1[i]).astype(BF16)
        out[0, :, i * HD : (i + 1) * HD] = rows[:SEQS]
        out[1, :, i * HD : (i + 1) * HD] = rows[SEQS:]

    for phase, src in ((0, send_a), (1, send_b), (2, recv_c)):
        whole(src.at[rest], send_sem.at[phase]).wait()
    whole(recv_t.at[pl.ds(1, tensors - 1)], send_sem.at[5]).wait()

    @pl.when(jnp.logical_not(same(there)))
    def _():
        whole(new_1, send_sem.at[4]).wait()

    @pl.when(column != t)
    def _():
        whole(send_d, send_sem.at[3]).wait()

    @pl.when(column == t)
    def _():
        whole(send_d.at[rest], send_sem.at[3]).wait()


def solution(mesh):
    groups, tensors = mesh.shape["group"], mesh.shape["tensor"]

    def per_device(tokens, queries, cache_kv, old_kv, new_kv, switch, lengths):
        depth = new_kv.shape[1]
        half = depth // 2
        block = tokens.shape[2] // tensors
        cache_len = cache_kv.shape[2]
        hbm = pl.BlockSpec(memory_space=pltpu.HBM)
        vmem = pltpu.VMEM
        result = pl.pallas_call(
            functools.partial(kernel, groups, tensors),
            out_shape=jax.ShapeDtypeStruct((STEPS, SEQS, block), BF16),
            in_specs=[hbm] * 7,
            out_specs=pl.BlockSpec(memory_space=vmem),
            scratch_shapes=[
                pltpu.SMEM(switch.shape, jnp.int32),
                pltpu.SMEM(lengths.shape, jnp.int32),
                vmem(tokens.shape, BF16),
                vmem((STEPS, SEQS, block), BF16),
                vmem(queries.shape, BF16),
                vmem((LAYERS, 2, cache_len, 2 * HD), BF16),
                vmem((LAYERS, 2, SHORT, 2 * HD), BF16),
                vmem((depth, 2 * HD), BF16),
                vmem(old_kv.shape[1:], BF16),
                vmem((depth, 2 * HD), BF16),
                vmem((depth, 2 * HD), BF16),
                vmem((groups, 2 * ROWS, half), BF16),
                vmem((groups, 2 * ROWS, half), BF16),
                vmem((groups, ROWS, 2 * HD), F32),
                vmem((groups, ROWS, 2 * HD), F32),
                vmem((2, 2 * ROWS, half), BF16),
                vmem((groups, 2 * ROWS, half), BF16),
                vmem((tensors, 2, 2 * ROWS, half), BF16),
                vmem((groups, ROWS, 2 * HD), F32),
                vmem((groups, ROWS, 2 * HD), F32),
                pltpu.SemaphoreType.DMA((8,)),
                pltpu.SemaphoreType.DMA((LAYERS, 2)),
                pltpu.SemaphoreType.DMA((LAYERS, 2)),
                pltpu.SemaphoreType.DMA((6,)),
                pltpu.SemaphoreType.DMA((6,)),
                pltpu.SemaphoreType.REGULAR,
                pltpu.SemaphoreType.REGULAR,
            ],
            compiler_params=pltpu.CompilerParams(
                collective_id=0, has_side_effects=True, vmem_limit_bytes=56 * 2**20
            ),
        )(tokens, queries, cache_kv, old_kv, new_kv, switch, lengths)
        return result

    return jax.shard_map(
        per_device,
        mesh=mesh,
        in_specs=(
            P(None, "group", None),
            P(None, None, "group", "tensor"),
            P(None, "group", None, "tensor"),
            P(None, None, "tensor"),
            P(None, "group", "tensor"),
            P(),
            P("group"),
        ),
        out_specs=P(None, "group", "tensor"),
        check_vma=False,
    )
```

```python
import functools
import math

import jax
import jax.numpy as jnp
from jax import lax
from jax.experimental import pallas as pl
from jax.experimental.pallas import tpu as pltpu
from jax.sharding import PartitionSpec as P

MESH = pl.DeviceIdType.MESH
F32, BF16 = jnp.float32, jnp.bfloat16
HD = 128
QPK = 8
LAYERS = 2
STEPS = 2
SEQS = 4
ROWS = STEPS * SEQS
SHORT = 16
FAR = -1e30
UNIT = HD**-0.5 * math.log2(math.e)


def stack_rows(ref_value):
    wide = ref_value.astype(F32)
    return jnp.concatenate([wide[0], wide[1]], axis=0)


def kernel(
    groups,
    tensors,
    tokens,
    queries,
    cache,
    old_kv,
    new_kv,
    switch_hbm,
    lengths_hbm,
    out,
    switch,
    lengths,
    tok_v,
    own_v,
    q_v,
    long_v,
    short_v,
    old_0,
    old_1,
    new_0,
    new_1,
    send_a,
    recv_a,
    send_b,
    recv_b,
    send_c,
    recv_c,
    recv_t,
    send_d,
    recv_d,
    load_sem,
    long_sem,
    short_sem,
    send_sem,
    recv_sem,
    near_sem,
    far_sem,
):
    g = lax.axis_index("group")
    t = lax.axis_index("tensor")
    depth = new_kv.shape[1]
    half = depth // 2
    width = tokens.shape[2]
    block = width // tensors
    x, y, core = g // 4, lax.rem(g // 2, 2), lax.rem(g, 2)

    def device(group, tensor):
        return {"group": group, "tensor": tensor}

    def holder(row_block, column_block):
        side = lax.rem(row_block, 2)
        across = lax.rem(row_block // 4 + column_block // 2 + 2 * side, 4)
        along = lax.rem(row_block // 2 + column_block + side, 2)
        return 4 * across + 2 * along + side

    def route(side):
        goes = device(holder(2 * (g // 2) + side, t), g // 2)
        return goes, 2 * lax.rem(x + 8 - t // 2 - 2 * side, 4) + lax.rem(y + t + side, 2)

    def targets(side):
        goes, columns = route(side)
        yield goes
        for group in range(groups):
            yield device(group, columns)

    there, column = route(core)
    origin = device(2 * t + core, column)

    def same(other):
        return (other["group"] == g) & (other["tensor"] == t)

    barrier = pltpu.get_barrier_semaphore()
    mate = device(g + 1 - 2 * core, t)

    def greet(other):
        pl.semaphore_signal(barrier, inc=1, device_id=other, device_id_type=MESH)

    def same_chip(other):
        return (other["group"] // 2 == g // 2) & (other["tensor"] == t)

    def senders():
        yield origin
        for block_index in range(groups):
            yield device(holder(block_index, t), block_index // 2)

    for k in range(1, groups // 2):
        greet(device(2 * lax.rem(g // 2 + k, groups // 2), t))

    @pl.when(core == 1)
    def _():
        greet(mate)

    for k in range(1, tensors):
        greet(device(g - core + 1, lax.rem(t + k, tensors)))
    for other in senders():

        @pl.when(jnp.logical_not(same_chip(other)))
        def _():
            greet(device(2 * (other["group"] // 2) + 1, other["tensor"]))

    loads = [
        pltpu.make_async_copy(tokens, tok_v, load_sem.at[0]),
        pltpu.make_async_copy(
            tokens.at[:, :, pl.ds(pl.multiple_of(t * block, block), block)],
            own_v,
            load_sem.at[1],
        ),
        pltpu.make_async_copy(queries, q_v, load_sem.at[2]),
        pltpu.make_async_copy(new_kv.at[0], new_0, load_sem.at[3]),
        pltpu.make_async_copy(
            old_kv.at[0, pl.ds(pl.multiple_of(g * depth, depth), depth), :],
            old_0,
            load_sem.at[4],
        ),
        pltpu.make_async_copy(switch_hbm, switch, load_sem.at[5]),
        pltpu.make_async_copy(lengths_hbm, lengths, load_sem.at[6]),
    ]
    late = pltpu.make_async_copy(old_kv.at[1], old_1, load_sem.at[7])
    longs = [
        [
            pltpu.make_async_copy(
                cache.at[layer, 2 * j], long_v.at[layer, j], long_sem.at[layer, j]
            )
            for j in range(2)
        ]
        for layer in range(LAYERS)
    ]
    shorts = [
        [
            pltpu.make_async_copy(
                cache.at[layer, 2 * j + 1, pl.ds(0, SHORT)],
                short_v.at[layer, j],
                short_sem.at[layer, j],
            )
            for j in range(2)
        ]
        for layer in range(LAYERS)
    ]
    for copy in loads:
        copy.start()
    for layer in range(LAYERS):
        for j in range(2):
            longs[layer][j].start()
            shorts[layer][j].start()
    late.start()

    loads[0].wait()
    mine = stack_rows(tok_v[...])
    for k in range(groups):
        piece = mine[:, k * depth : (k + 1) * depth]
        send_a[k] = jnp.concatenate([piece[:, :half], piece[:, half:]], axis=0).astype(BF16)
    scale_0 = lax.rsqrt(jnp.sum(mine * mine, axis=1, keepdims=True) / width + 1e-05)

    @pl.when(core == 0)
    def _():
        pl.semaphore_wait(barrier, groups - 1)
        pl.semaphore_signal(near_sem, inc=1, device_id=mate, device_id_type=MESH)

    @pl.when(core == 1)
    def _():
        pl.semaphore_wait(near_sem, 1)

    def far_barrier():
        count = 2 * (tensors - 1)
        for other_core in range(2):
            for other in targets(other_core):
                count = count + jnp.logical_not(same_chip(other)).astype(jnp.int32)

        @pl.when(core == 1)
        def _():
            pl.semaphore_wait(barrier, count)
            pl.semaphore_signal(far_sem, inc=1, device_id=mate, device_id_type=MESH)

        @pl.when(core == 0)
        def _():
            pl.semaphore_wait(far_sem, 1)

    def whole(ref, sem):
        return pltpu.make_async_copy(ref, ref, sem)

    def to_group(src, dst, phase, sign, by_slot):
        for k in range(1, groups):
            peer = lax.rem(g + (groups + sign * k), groups)
            pltpu.make_async_remote_copy(
                src_ref=src.at[k if by_slot else peer],
                dst_ref=dst.at[k],
                send_sem=send_sem.at[phase],
                recv_sem=recv_sem.at[phase],
                device_id={"group": peer, "tensor": t},
                device_id_type=MESH,
            ).start()

    to_group(send_a, recv_a, 0, 1, False)
    recv_a[0] = send_a[g]

    def put(src, dst, other, phase):
        @pl.when(jnp.logical_not(same(other)))
        def _():
            pltpu.make_async_remote_copy(
                src_ref=src,
                dst_ref=dst,
                send_sem=send_sem.at[phase],
                recv_sem=recv_sem.at[phase],
                device_id=other,
                device_id_type=MESH,
            ).start()

        @pl.when(same(other))
        def _():
            pltpu.make_async_copy(src, dst, recv_sem.at[phase]).start()

    far_barrier()
    put(new_kv.at[1], new_1, there, 4)

    row = lax.broadcasted_iota(jnp.int32, (QPK * ROWS, 1), 0)
    row_seq = lax.rem(row, SEQS)

    def stale(layer):
        every = stack_rows(q_v[:, layer])
        q = jnp.concatenate([every[:, i * HD : (i + 1) * HD] for i in range(QPK)], axis=0)
        q16 = q.astype(BF16)
        scores = []
        blocks = []
        for j in range(2):
            longs[layer][j].wait()
            shorts[layer][j].wait()
            for held, seq in ((long_v, 2 * j), (short_v, 2 * j + 1)):
                s = lax.dot_general(
                    q16, held[layer, j, :, :HD], (((1,), (1,)), ((), ())), preferred_element_type=F32
                )
                col = lax.broadcasted_iota(jnp.int32, s.shape, 1)
                keep = (col < lengths[seq]) & (row_seq == seq)
                scores.append(jnp.where(keep, s * UNIT, FAR))
                blocks.append((held, j))
        top = functools.reduce(
            jnp.maximum, [jnp.max(s, axis=1, keepdims=True) for s in scores]
        )
        total = jnp.zeros_like(top)
        mixed = jnp.zeros((QPK * ROWS, HD), F32)
        for s, (held, j) in zip(scores, blocks):
            weight = jnp.exp2(s - top)
            total = total + jnp.sum(weight, axis=1, keepdims=True)
            mixed = mixed + jnp.dot(weight.astype(BF16), held[layer, j, :, HD:], preferred_element_type=F32)
        shape = (QPK, ROWS)
        return (
            q.reshape(*shape, HD),
            top.reshape(*shape, 1),
            total.reshape(*shape, 1),
            mixed.reshape(*shape, HD),
        )

    upper = lax.broadcasted_iota(jnp.int32, (ROWS, HD), 0) < SEQS

    def by_step(fresh):
        other = jnp.concatenate([fresh[SEQS:], fresh[:SEQS]], axis=0)
        return jnp.where(upper, fresh, other), jnp.where(upper, other, fresh)

    def merge(key, value, part):
        q, top, total, mixed = part
        key_0, key_1 = by_step(key.astype(BF16).astype(F32))
        value_0, value_1 = by_step(value.astype(BF16).astype(F32))
        s_0 = jnp.sum(q * key_0[None], axis=2, keepdims=True) * UNIT
        s_1 = jnp.sum(q * key_1[None], axis=2, keepdims=True) * UNIT
        s_1 = jnp.where(upper[None, :, :1], FAR, s_1)
        peak = jnp.maximum(top, jnp.maximum(s_0, s_1))
        keep = jnp.exp2(top - peak)
        w_0 = jnp.exp2(s_0 - peak)
        w_1 = jnp.exp2(s_1 - peak)
        norm = 1.0 / (total * keep + w_0 + w_1)
        result = (mixed * keep + w_0 * value_0[None] + w_1 * value_1[None]) * norm
        return result.astype(BF16).astype(F32)

    def fold(products):
        products = products.reshape(groups, ROWS, 2 * HD)
        return jnp.concatenate([products[:, :, :HD], products[:, :, HD:]], axis=1).astype(BF16)

    def flatten(features):
        return jnp.concatenate(
            [features[:, :ROWS].reshape(-1, half), features[:, ROWS:].reshape(-1, half)], axis=1
        ).astype(BF16)

    for copy in loads[1:]:
        copy.wait()
    part_0 = stale(0)

    rest = pl.ds(1, groups - 1)
    whole(recv_a.at[rest], recv_sem.at[0]).wait()
    flat = flatten(recv_a[...].astype(F32))
    by_new = jnp.dot(flat, new_0[...], preferred_element_type=F32)
    by_old = jnp.dot(flat, old_0[...], preferred_element_type=F32)
    step = lax.rem(lax.broadcasted_iota(jnp.int32, by_new.shape, 0), ROWS) // SEQS
    send_b[...] = fold(jnp.where(step >= switch[0], by_new, by_old))
    to_group(send_b, recv_b, 1, -1, True)
    recv_b[0] = send_b[0]
    part_1 = stale(1)

    whole(recv_b.at[rest], recv_sem.at[1]).wait()
    summed = jnp.sum(recv_b[...].astype(F32), axis=0)
    attended_0 = merge(summed[:ROWS] * scale_0, summed[ROWS:] * scale_0, part_0)
    own = stack_rows(own_v[...])
    hidden = [own[:, i * HD : (i + 1) * HD] + attended_0[i] for i in range(QPK)]
    for h in range(2):
        send_c[h] = jnp.concatenate(
            [jnp.concatenate(hidden[4 * h + 2 * r : 4 * h + 2 * r + 2], axis=1) for r in range(2)],
            axis=0,
        ).astype(BF16)

    for k in range(1, groups):
        peer = lax.rem(g + k, groups)
        pltpu.make_async_remote_copy(
            src_ref=send_c.at[lax.rem(peer, 2)],
            dst_ref=recv_c.at[g],
            send_sem=send_sem.at[2],
            recv_sem=recv_sem.at[2],
            device_id=device(peer, t),
            device_id_type=MESH,
        ).start()
    pltpu.make_async_copy(send_c.at[core], recv_c.at[g], recv_sem.at[2]).start()
    for k in range(1, tensors):
        pltpu.make_async_remote_copy(
            src_ref=send_c,
            dst_ref=recv_t.at[t],
            send_sem=send_sem.at[5],
            recv_sem=recv_sem.at[5],
            device_id=device(g, lax.rem(t + k, tensors)),
            device_id_type=MESH,
        ).start()
    pltpu.make_async_copy(send_c, recv_t.at[t], recv_sem.at[5]).start()

    whole(new_1, recv_sem.at[4]).wait()
    whole(recv_c, recv_sem.at[2]).wait()
    flat = flatten(recv_c[...].astype(F32))
    send_d[...] = fold(jnp.dot(flat, new_1[...], preferred_element_type=F32))
    for k in range(groups):
        peer = lax.rem(g + k, groups)
        put(send_d.at[peer], recv_d.at[2 * t + core], device(peer, column), 3)

    late.wait()
    whole(recv_t, recv_sem.at[5]).wait()
    parts = [recv_t[i, h].astype(F32) for i in range(tensors) for h in range(2)]
    wide = jnp.concatenate([part[at : at + ROWS] for part in parts for at in (0, ROWS)], axis=1)
    scale_1 = lax.rsqrt(jnp.sum(wide * wide, axis=1, keepdims=True) / width + 1e-05)
    by_old = jnp.dot(wide.astype(BF16), old_1[...], preferred_element_type=F32)
    use_new = lax.broadcasted_iota(jnp.int32, (ROWS, HD), 0) // SEQS >= switch[1]

    whole(recv_d, recv_sem.at[3]).wait()
    summed = jnp.sum(recv_d[...].astype(F32), axis=0)
    key = jnp.where(use_new, summed[:ROWS], by_old[:, :HD]) * scale_1
    value = jnp.where(use_new, summed[ROWS:], by_old[:, HD:]) * scale_1
    attended_1 = merge(key, value, part_1)
    for i in range(QPK):
        rows = (hidden[i] + attended_1[i]).astype(BF16)
        out[0, :, i * HD : (i + 1) * HD] = rows[:SEQS]
        out[1, :, i * HD : (i + 1) * HD] = rows[SEQS:]

    for phase, src in ((0, send_a), (1, send_b), (2, recv_c)):
        whole(src.at[rest], send_sem.at[phase]).wait()
    whole(recv_t.at[pl.ds(1, tensors - 1)], send_sem.at[5]).wait()

    @pl.when(jnp.logical_not(same(there)))
    def _():
        whole(new_1, send_sem.at[4]).wait()

    @pl.when(column != t)
    def _():
        whole(send_d, send_sem.at[3]).wait()

    @pl.when(column == t)
    def _():
        whole(send_d.at[rest], send_sem.at[3]).wait()


def solution(mesh):
    groups, tensors = mesh.shape["group"], mesh.shape["tensor"]

    def per_device(*operands):
        tokens, queries, cache_kv, old_kv, new_kv, switch, lengths = operands
        depth = new_kv.shape[1]
        half = depth // 2
        block = tokens.shape[2] // tensors
        cache_len = cache_kv.shape[2]
        hbm = pl.BlockSpec(memory_space=pltpu.HBM)
        vmem = pltpu.VMEM
        result = pl.pallas_call(
            functools.partial(kernel, groups, tensors),
            out_shape=jax.ShapeDtypeStruct((STEPS, SEQS, block), BF16),
            in_specs=[hbm] * 7,
            out_specs=pl.BlockSpec(memory_space=vmem),
            scratch_shapes=[
                pltpu.SMEM(switch.shape, jnp.int32),
                pltpu.SMEM(lengths.shape, jnp.int32),
                vmem(tokens.shape, BF16),
                vmem((STEPS, SEQS, block), BF16),
                vmem(queries.shape, BF16),
                vmem((LAYERS, 2, cache_len, 2 * HD), BF16),
                vmem((LAYERS, 2, SHORT, 2 * HD), BF16),
                vmem((depth, 2 * HD), BF16),
                vmem(old_kv.shape[1:], BF16),
                vmem((depth, 2 * HD), BF16),
                vmem((depth, 2 * HD), BF16),
                vmem((groups, 2 * ROWS, half), BF16),
                vmem((groups, 2 * ROWS, half), BF16),
                vmem((groups, 2 * ROWS, HD), BF16),
                vmem((groups, 2 * ROWS, HD), BF16),
                vmem((2, 2 * ROWS, half), BF16),
                vmem((groups, 2 * ROWS, half), BF16),
                vmem((tensors, 2, 2 * ROWS, half), BF16),
                vmem((groups, 2 * ROWS, HD), BF16),
                vmem((groups, 2 * ROWS, HD), BF16),
                pltpu.SemaphoreType.DMA((8,)),
                pltpu.SemaphoreType.DMA((LAYERS, 2)),
                pltpu.SemaphoreType.DMA((LAYERS, 2)),
                pltpu.SemaphoreType.DMA((6,)),
                pltpu.SemaphoreType.DMA((6,)),
                pltpu.SemaphoreType.REGULAR,
                pltpu.SemaphoreType.REGULAR,
            ],
            compiler_params=pltpu.CompilerParams(
                collective_id=0, has_side_effects=True, vmem_limit_bytes=40 * 2**20
            ),
        )(*[pltpu.with_memory_space_constraint(operand, pltpu.HBM) for operand in operands])
        return result

    return jax.shard_map(
        per_device,
        mesh=mesh,
        in_specs=(
            P(None, "group", None),
            P(None, None, "group", "tensor"),
            P(None, "group", None, "tensor"),
            P(None, None, "tensor"),
            P(None, "group", "tensor"),
            P(),
            P("group"),
        ),
        out_specs=P(None, "group", "tensor"),
        check_vma=False,
    )
```

```python
import functools
import math

import jax
import jax.numpy as jnp
from jax import lax
from jax.experimental import pallas as pl
from jax.experimental.pallas import tpu as pltpu
from jax.sharding import PartitionSpec as P

MESH = pl.DeviceIdType.MESH
F32, BF16 = jnp.float32, jnp.bfloat16
HD = 128
QPK = 8
LAYERS = 2
STEPS = 2
SEQS = 4
ROWS = STEPS * SEQS
SHORT = 16
FAR = -1e30
UNIT = HD**-0.5 * math.log2(math.e)


def stack_rows(ref_value):
    wide = ref_value.astype(F32)
    return jnp.concatenate([wide[0], wide[1]], axis=0)


def kernel(
    groups,
    tensors,
    tokens,
    queries,
    cache,
    old_kv,
    new_kv,
    switch_hbm,
    lengths_hbm,
    out,
    switch,
    lengths,
    tok_v,
    own_v,
    q_v,
    long_v,
    short_v,
    old_0,
    old_1,
    new_0,
    new_1,
    send_a,
    recv_a,
    send_b,
    recv_b,
    send_c,
    recv_c,
    recv_t,
    send_d,
    recv_d,
    load_sem,
    long_sem,
    short_sem,
    send_sem,
    recv_sem,
    near_sem,
    far_sem,
):
    g = lax.axis_index("group")
    t = lax.axis_index("tensor")
    depth = new_kv.shape[1]
    half = depth // 2
    width = tokens.shape[2]
    block = width // tensors
    x, y, core = g // 4, lax.rem(g // 2, 2), lax.rem(g, 2)

    def device(group, tensor):
        return {"group": group, "tensor": tensor}

    def holder(row_block, column_block):
        across = lax.rem(row_block // 4 + column_block + 1, 4)
        along = lax.rem(row_block // 2 + column_block // 4 + column_block, 2)
        return 4 * across + 2 * along + lax.rem(row_block, 2)

    def route(side):
        goes = device(holder(2 * (g // 2) + side, t), g // 2)
        low = lax.rem(x + 7 - t // 2, 4)
        return goes, 4 * lax.rem(y + t + low, 2) + low

    def targets(side):
        goes, columns = route(side)
        yield goes
        for group in range(groups):
            yield device(group, columns)

    there, column = route(core)
    origin = device(2 * t + core, column)

    def same(other):
        return (other["group"] == g) & (other["tensor"] == t)

    barrier = pltpu.get_barrier_semaphore()
    mate = device(g + 1 - 2 * core, t)

    def greet(other):
        pl.semaphore_signal(barrier, inc=1, device_id=other, device_id_type=MESH)

    def same_chip(other):
        return (other["group"] // 2 == g // 2) & (other["tensor"] == t)

    def senders():
        yield origin
        for block_index in range(groups):
            yield device(holder(block_index, t), block_index // 2)

    for k in range(1, groups // 2):
        greet(device(2 * lax.rem(g // 2 + k, groups // 2), t))

    @pl.when(core == 1)
    def _():
        greet(mate)

    for k in range(1, tensors):
        greet(device(g - core + 1, lax.rem(t + k, tensors)))
    for other in senders():

        @pl.when(jnp.logical_not(same_chip(other)))
        def _():
            greet(device(2 * (other["group"] // 2) + 1, other["tensor"]))

    loads = [
        pltpu.make_async_copy(tokens, tok_v, load_sem.at[0]),
        pltpu.make_async_copy(
            tokens.at[:, :, pl.ds(pl.multiple_of(t * block, block), block)],
            own_v,
            load_sem.at[1],
        ),
        pltpu.make_async_copy(queries, q_v, load_sem.at[2]),
        pltpu.make_async_copy(new_kv.at[0], new_0, load_sem.at[3]),
        pltpu.make_async_copy(
            old_kv.at[0, pl.ds(pl.multiple_of(g * depth, depth), depth), :],
            old_0,
            load_sem.at[4],
        ),
        pltpu.make_async_copy(switch_hbm, switch, load_sem.at[5]),
        pltpu.make_async_copy(lengths_hbm, lengths, load_sem.at[6]),
    ]
    late = pltpu.make_async_copy(old_kv.at[1], old_1, load_sem.at[7])
    longs = [
        [
            pltpu.make_async_copy(
                cache.at[layer, 2 * j], long_v.at[layer, j], long_sem.at[layer, j]
            )
            for j in range(2)
        ]
        for layer in range(LAYERS)
    ]
    shorts = [
        [
            pltpu.make_async_copy(
                cache.at[layer, 2 * j + 1, pl.ds(0, SHORT)],
                short_v.at[layer, j],
                short_sem.at[layer, j],
            )
            for j in range(2)
        ]
        for layer in range(LAYERS)
    ]
    for copy in loads:
        copy.start()

    loads[0].wait()
    mine = stack_rows(tok_v[...])
    for k in range(groups):
        piece = mine[:, k * depth : (k + 1) * depth]
        send_a[k] = jnp.concatenate([piece[:, :half], piece[:, half:]], axis=0).astype(BF16)
    scale_0 = lax.rsqrt(jnp.sum(mine * mine, axis=1, keepdims=True) / width + 1e-05)

    @pl.when(core == 0)
    def _():
        pl.semaphore_wait(barrier, groups - 1)
        pl.semaphore_signal(near_sem, inc=1, device_id=mate, device_id_type=MESH)

    @pl.when(core == 1)
    def _():
        pl.semaphore_wait(near_sem, 1)

    def far_barrier():
        count = 2 * (tensors - 1)
        for other_core in range(2):
            for other in targets(other_core):
                count = count + jnp.logical_not(same_chip(other)).astype(jnp.int32)

        @pl.when(core == 1)
        def _():
            pl.semaphore_wait(barrier, count)
            pl.semaphore_signal(far_sem, inc=1, device_id=mate, device_id_type=MESH)

        @pl.when(core == 0)
        def _():
            pl.semaphore_wait(far_sem, 1)

    def whole(ref, sem):
        return pltpu.make_async_copy(ref, ref, sem)

    steps = [
        (along_x, along_y, along_core)
        for along_x, along_y in ((2, 1), (2, 0), (1, 1), (3, 1), (1, 0), (3, 0), (0, 1), (0, 0))
        for along_core in (1, 0)
    ][:-1]

    def step_from(sign, step):
        along_x, along_y, along_core = step
        return (
            4 * lax.rem(x + 4 + sign * along_x, 4)
            + 2 * lax.rem(y + along_y, 2)
            + lax.rem(core + along_core, 2)
        )

    def to_group(src, dst, phase, sign, by_slot):
        for k, step in enumerate(steps, 1):
            peer = step_from(sign, step)
            pltpu.make_async_remote_copy(
                src_ref=src.at[k if by_slot else peer],
                dst_ref=dst.at[k],
                send_sem=send_sem.at[phase],
                recv_sem=recv_sem.at[phase],
                device_id={"group": peer, "tensor": t},
                device_id_type=MESH,
            ).start()

    to_group(send_a, recv_a, 0, 1, False)
    recv_a[0] = send_a[g]

    def put(src, dst, other, phase):
        @pl.when(jnp.logical_not(same(other)))
        def _():
            pltpu.make_async_remote_copy(
                src_ref=src,
                dst_ref=dst,
                send_sem=send_sem.at[phase],
                recv_sem=recv_sem.at[phase],
                device_id=other,
                device_id_type=MESH,
            ).start()

        @pl.when(same(other))
        def _():
            pltpu.make_async_copy(src, dst, recv_sem.at[phase]).start()

    for layer in range(LAYERS):
        for j in range(2):
            longs[layer][j].start()
            shorts[layer][j].start()
    late.start()
    far_barrier()
    put(new_kv.at[1, pl.ds(0,320)], new_1.at[pl.ds(0,320)], there, 4)

    row = lax.broadcasted_iota(jnp.int32, (QPK * ROWS, 1), 0)
    row_seq = lax.rem(row, SEQS)

    def stale(layer):
        every = stack_rows(q_v[:, layer])
        q = jnp.concatenate([every[:, i * HD : (i + 1) * HD] for i in range(QPK)], axis=0)
        q16 = q.astype(BF16)
        scores = []
        blocks = []
        for j in range(2):
            longs[layer][j].wait()
            shorts[layer][j].wait()
            for held, seq in ((long_v, 2 * j), (short_v, 2 * j + 1)):
                s = lax.dot_general(
                    q16, held[layer, j, :, :HD], (((1,), (1,)), ((), ())), preferred_element_type=F32
                )
                col = lax.broadcasted_iota(jnp.int32, s.shape, 1)
                keep = (col < lengths[seq]) & (row_seq == seq)
                scores.append(jnp.where(keep, s * UNIT, FAR))
                blocks.append((held, j))
        top = functools.reduce(
            jnp.maximum, [jnp.max(s, axis=1, keepdims=True) for s in scores]
        )
        total = jnp.zeros_like(top)
        mixed = jnp.zeros((QPK * ROWS, HD), F32)
        for s, (held, j) in zip(scores, blocks):
            weight = jnp.exp2(s - top)
            total = total + jnp.sum(weight, axis=1, keepdims=True)
            mixed = mixed + jnp.dot(weight.astype(BF16), held[layer, j, :, HD:], preferred_element_type=F32)
        shape = (QPK, ROWS)
        return (
            q.reshape(*shape, HD),
            top.reshape(*shape, 1),
            total.reshape(*shape, 1),
            mixed.reshape(*shape, HD),
        )

    upper = lax.broadcasted_iota(jnp.int32, (ROWS, HD), 0) < SEQS

    def by_step(fresh):
        other = jnp.concatenate([fresh[SEQS:], fresh[:SEQS]], axis=0)
        return jnp.where(upper, fresh, other), jnp.where(upper, other, fresh)

    def merge(key, value, part):
        q, top, total, mixed = part
        key_0, key_1 = by_step(key.astype(BF16).astype(F32))
        value_0, value_1 = by_step(value.astype(BF16).astype(F32))
        s_0 = jnp.sum(q * key_0[None], axis=2, keepdims=True) * UNIT
        s_1 = jnp.sum(q * key_1[None], axis=2, keepdims=True) * UNIT
        s_1 = jnp.where(upper[None, :, :1], FAR, s_1)
        peak = jnp.maximum(top, jnp.maximum(s_0, s_1))
        keep = jnp.exp2(top - peak)
        w_0 = jnp.exp2(s_0 - peak)
        w_1 = jnp.exp2(s_1 - peak)
        norm = 1.0 / (total * keep + w_0 + w_1)
        result = (mixed * keep + w_0 * value_0[None] + w_1 * value_1[None]) * norm
        return result.astype(BF16).astype(F32)

    def fold(products):
        products = products.reshape(groups, ROWS, 2 * HD)
        return jnp.concatenate([products[:, :, :HD], products[:, :, HD:]], axis=1).astype(BF16)

    def flatten(features):
        return jnp.concatenate(
            [features[:, :ROWS].reshape(-1, half), features[:, ROWS:].reshape(-1, half)], axis=1
        ).astype(BF16)

    for copy in loads[1:]:
        copy.wait()
    part_0 = stale(0)

    rest = pl.ds(1, groups - 1)
    whole(recv_a.at[rest], recv_sem.at[0]).wait()
    flat = flatten(recv_a[...].astype(F32))
    by_new = jnp.dot(flat, new_0[...], preferred_element_type=F32)
    by_old = jnp.dot(flat, old_0[...], preferred_element_type=F32)
    row_step = lax.rem(lax.broadcasted_iota(jnp.int32, by_new.shape, 0), ROWS) // SEQS
    send_b[...] = fold(jnp.where(row_step >= switch[0], by_new, by_old))
    to_group(send_b, recv_b, 1, -1, True)
    put(new_kv.at[1, pl.ds(320,192)], new_1.at[pl.ds(320,192)], there, 4)
    recv_b[0] = send_b[0]
    part_1 = stale(1)

    own = stack_rows(own_v[...])
    whole(recv_b.at[rest], recv_sem.at[1]).wait()
    summed = jnp.sum(recv_b[...].astype(F32), axis=0)
    attended_0 = merge(summed[:ROWS] * scale_0, summed[ROWS:] * scale_0, part_0)
    hidden = [own[:, i * HD : (i + 1) * HD] + attended_0[i] for i in range(QPK)]
    for h in range(2):
        send_c[h] = jnp.concatenate(
            [jnp.concatenate(hidden[4 * h + 2 * r : 4 * h + 2 * r + 2], axis=1) for r in range(2)],
            axis=0,
        ).astype(BF16)

    for step in steps:
        peer = step_from(1, step)
        pltpu.make_async_remote_copy(
            src_ref=send_c.at[lax.rem(core + step[2], 2)],
            dst_ref=recv_c.at[g],
            send_sem=send_sem.at[2],
            recv_sem=recv_sem.at[2],
            device_id=device(peer, t),
            device_id_type=MESH,
        ).start()
    pltpu.make_async_copy(send_c.at[core], recv_c.at[g], recv_sem.at[2]).start()
    for k in range(1, tensors):
        pltpu.make_async_remote_copy(
            src_ref=send_c,
            dst_ref=recv_t.at[t],
            send_sem=send_sem.at[5],
            recv_sem=recv_sem.at[5],
            device_id=device(g, lax.rem(t + k, tensors)),
            device_id_type=MESH,
        ).start()
    pltpu.make_async_copy(send_c, recv_t.at[t], recv_sem.at[5]).start()

    whole(new_1, recv_sem.at[4]).wait()
    whole(recv_c, recv_sem.at[2]).wait()
    flat = flatten(recv_c[...].astype(F32))
    send_d[...] = fold(jnp.dot(flat, new_1[...], preferred_element_type=F32))
    for peer in (1, 0, 3, 2, 13, 12, 5, 4, 15, 14, 7, 6, 9, 8, 11, 10):
        put(send_d.at[peer], recv_d.at[2 * t + core], device(peer, column), 3)

    late.wait()
    whole(recv_t, recv_sem.at[5]).wait()
    parts = [recv_t[i, h].astype(F32) for i in range(tensors) for h in range(2)]
    wide = jnp.concatenate([part[at : at + ROWS] for part in parts for at in (0, ROWS)], axis=1)
    scale_1 = lax.rsqrt(jnp.sum(wide * wide, axis=1, keepdims=True) / width + 1e-05)
    by_old = jnp.dot(wide.astype(BF16), old_1[...], preferred_element_type=F32)
    use_new = lax.broadcasted_iota(jnp.int32, (ROWS, HD), 0) // SEQS >= switch[1]

    whole(recv_d, recv_sem.at[3]).wait()
    summed = jnp.sum(recv_d[...].astype(F32), axis=0)
    key = jnp.where(use_new, summed[:ROWS], by_old[:, :HD]) * scale_1
    value = jnp.where(use_new, summed[ROWS:], by_old[:, HD:]) * scale_1
    attended_1 = merge(key, value, part_1)
    for i in range(QPK):
        rows = (hidden[i] + attended_1[i]).astype(BF16)
        out[0, :, i * HD : (i + 1) * HD] = rows[:SEQS]
        out[1, :, i * HD : (i + 1) * HD] = rows[SEQS:]

    for phase, src in ((0, send_a), (1, send_b), (2, recv_c)):
        whole(src.at[rest], send_sem.at[phase]).wait()
    whole(recv_t.at[pl.ds(1, tensors - 1)], send_sem.at[5]).wait()

    @pl.when(jnp.logical_not(same(there)))
    def _():
        whole(new_1, send_sem.at[4]).wait()

    @pl.when(column != t)
    def _():
        whole(send_d, send_sem.at[3]).wait()

    @pl.when(column == t)
    def _():
        whole(send_d.at[rest], send_sem.at[3]).wait()


def solution(mesh):
    groups, tensors = mesh.shape["group"], mesh.shape["tensor"]

    def per_device(*operands):
        tokens, queries, cache_kv, old_kv, new_kv, switch, lengths = operands
        depth = new_kv.shape[1]
        half = depth // 2
        block = tokens.shape[2] // tensors
        cache_len = cache_kv.shape[2]
        hbm = pl.BlockSpec(memory_space=pltpu.HBM)
        vmem = pltpu.VMEM
        result = pl.pallas_call(
            functools.partial(kernel, groups, tensors),
            out_shape=jax.ShapeDtypeStruct((STEPS, SEQS, block), BF16),
            in_specs=[hbm] * 7,
            out_specs=pl.BlockSpec(memory_space=vmem),
            scratch_shapes=[
                pltpu.SMEM(switch.shape, jnp.int32),
                pltpu.SMEM(lengths.shape, jnp.int32),
                vmem(tokens.shape, BF16),
                vmem((STEPS, SEQS, block), BF16),
                vmem(queries.shape, BF16),
                vmem((LAYERS, 2, cache_len, 2 * HD), BF16),
                vmem((LAYERS, 2, SHORT, 2 * HD), BF16),
                vmem((depth, 2 * HD), BF16),
                vmem(old_kv.shape[1:], BF16),
                vmem((depth, 2 * HD), BF16),
                vmem((depth, 2 * HD), BF16),
                vmem((groups, 2 * ROWS, half), BF16),
                vmem((groups, 2 * ROWS, half), BF16),
                vmem((groups, 2 * ROWS, HD), BF16),
                vmem((groups, 2 * ROWS, HD), BF16),
                vmem((2, 2 * ROWS, half), BF16),
                vmem((groups, 2 * ROWS, half), BF16),
                vmem((tensors, 2, 2 * ROWS, half), BF16),
                vmem((groups, 2 * ROWS, HD), BF16),
                vmem((groups, 2 * ROWS, HD), BF16),
                pltpu.SemaphoreType.DMA((8,)),
                pltpu.SemaphoreType.DMA((LAYERS, 2)),
                pltpu.SemaphoreType.DMA((LAYERS, 2)),
                pltpu.SemaphoreType.DMA((6,)),
                pltpu.SemaphoreType.DMA((6,)),
                pltpu.SemaphoreType.REGULAR,
                pltpu.SemaphoreType.REGULAR,
            ],
            compiler_params=pltpu.CompilerParams(
                collective_id=0, has_side_effects=True, vmem_limit_bytes=40 * 2**20
            ),
        )(*[pltpu.with_memory_space_constraint(operand, pltpu.HBM) for operand in operands])
        return result

    return jax.shard_map(
        per_device,
        mesh=mesh,
        in_specs=(
            P(None, "group", None),
            P(None, None, "group", "tensor"),
            P(None, "group", None, "tensor"),
            P(None, None, "tensor"),
            P(None, "group", "tensor"),
            P(),
            P("group"),
        ),
        out_specs=P(None, "group", "tensor"),
        check_vma=False,
    )
```

```python
import functools
import math

import jax
import jax.numpy as jnp
from jax import lax
from jax.experimental import pallas as pl
from jax.experimental.pallas import tpu as pltpu
from jax.sharding import PartitionSpec as P

MESH = pl.DeviceIdType.MESH
F32, BF16 = jnp.float32, jnp.bfloat16
HD = 128
QPK = 8
LAYERS = 2
STEPS = 2
SEQS = 4
ROWS = STEPS * SEQS
SHORT = 16
FAR = -1e30
UNIT = HD**-0.5 * math.log2(math.e)


def stack_rows(ref_value):
    wide = ref_value.astype(F32)
    return jnp.concatenate([wide[0], wide[1]], axis=0)


def kernel(
    groups,
    tensors,
    tokens,
    queries,
    cache,
    old_kv,
    new_kv,
    switch_hbm,
    lengths_hbm,
    out,
    switch,
    lengths,
    tok_v,
    own_v,
    q_v,
    long_v,
    short_v,
    old_0,
    old_1,
    new_0,
    new_1,
    send_a,
    recv_a,
    send_b,
    recv_b,
    send_c,
    recv_c,
    recv_t,
    send_d,
    recv_d,
    load_sem,
    long_sem,
    short_sem,
    send_sem,
    recv_sem,
    near_sem,
    far_sem,
):
    g = lax.axis_index("group")
    t = lax.axis_index("tensor")
    depth = new_kv.shape[1]
    half = depth // 2
    width = tokens.shape[2]
    block = width // tensors
    x, y, core = g // 4, lax.rem(g // 2, 2), lax.rem(g, 2)

    def device(group, tensor):
        return {"group": group, "tensor": tensor}

    def holder(row_block, column_block):
        across = lax.rem(row_block // 4 + column_block + 1, 4)
        along = lax.rem(row_block // 2 + column_block // 4 + column_block, 2)
        return 4 * across + 2 * along + lax.rem(row_block, 2)

    def route(side):
        goes = device(holder(2 * (g // 2) + side, t), g // 2)
        low = lax.rem(x + 7 - t // 2, 4)
        return goes, 4 * lax.rem(y + t + low, 2) + low

    def targets(side):
        goes, columns = route(side)
        yield goes
        for group in range(groups):
            yield device(group, columns)

    there, column = route(core)
    origin = device(2 * t + core, column)

    def same(other):
        return (other["group"] == g) & (other["tensor"] == t)

    barrier = pltpu.get_barrier_semaphore()
    mate = device(g + 1 - 2 * core, t)

    def greet(other):
        pl.semaphore_signal(barrier, inc=1, device_id=other, device_id_type=MESH)

    def same_chip(other):
        return (other["group"] // 2 == g // 2) & (other["tensor"] == t)

    def senders():
        yield origin
        for block_index in range(groups):
            yield device(holder(block_index, t), block_index // 2)

    for k in range(1, groups // 2):
        greet(device(2 * lax.rem(g // 2 + k, groups // 2), t))

    @pl.when(core == 1)
    def _():
        greet(mate)

    load_tokens = pltpu.make_async_copy(tokens, tok_v, load_sem.at[0])
    load_tokens.start()

    for k in range(1, tensors):
        greet(device(g - core + 1, lax.rem(t + k, tensors)))
    for other in senders():

        @pl.when(jnp.logical_not(same_chip(other)))
        def _():
            greet(device(2 * (other["group"] // 2) + 1, other["tensor"]))

    loads = [
        load_tokens,
        pltpu.make_async_copy(
            tokens.at[:, :, pl.ds(pl.multiple_of(t * block, block), block)],
            own_v,
            load_sem.at[1],
        ),
        pltpu.make_async_copy(queries, q_v, load_sem.at[2]),
        pltpu.make_async_copy(new_kv.at[0], new_0, load_sem.at[3]),
        pltpu.make_async_copy(
            old_kv.at[0, pl.ds(pl.multiple_of(g * depth, depth), depth), :],
            old_0,
            load_sem.at[4],
        ),
        pltpu.make_async_copy(switch_hbm, switch, load_sem.at[5]),
        pltpu.make_async_copy(lengths_hbm, lengths, load_sem.at[6]),
    ]
    late = pltpu.make_async_copy(old_kv.at[1], old_1, load_sem.at[7])
    longs = [
        [
            pltpu.make_async_copy(
                cache.at[layer, 2 * j], long_v.at[layer, j], long_sem.at[layer, j]
            )
            for j in range(2)
        ]
        for layer in range(LAYERS)
    ]
    shorts = [
        [
            pltpu.make_async_copy(
                cache.at[layer, 2 * j + 1, pl.ds(0, SHORT)],
                short_v.at[layer, j],
                short_sem.at[layer, j],
            )
            for j in range(2)
        ]
        for layer in range(LAYERS)
    ]
    for copy in loads[1:]:
        copy.start()

    loads[0].wait()
    mine = stack_rows(tok_v[...])
    for k in range(groups):
        piece = mine[:, k * depth : (k + 1) * depth]
        send_a[k] = jnp.concatenate([piece[:, :half], piece[:, half:]], axis=0).astype(BF16)
    scale_0 = lax.rsqrt(jnp.sum(mine * mine, axis=1, keepdims=True) / width + 1e-05)

    @pl.when(core == 0)
    def _():
        pl.semaphore_wait(barrier, groups - 1)
        pl.semaphore_signal(near_sem, inc=1, device_id=mate, device_id_type=MESH)

    @pl.when(core == 1)
    def _():
        pl.semaphore_wait(near_sem, 1)

    def far_barrier():
        count = 2 * (tensors - 1)
        for other_core in range(2):
            for other in targets(other_core):
                count = count + jnp.logical_not(same_chip(other)).astype(jnp.int32)

        @pl.when(core == 1)
        def _():
            pl.semaphore_wait(barrier, count)
            pl.semaphore_signal(far_sem, inc=1, device_id=mate, device_id_type=MESH)

        @pl.when(core == 0)
        def _():
            pl.semaphore_wait(far_sem, 1)

    def whole(ref, sem):
        return pltpu.make_async_copy(ref, ref, sem)

    steps = [
        (along_x, along_y, along_core)
        for along_x, along_y in ((2, 1), (2, 0), (1, 1), (3, 1), (1, 0), (3, 0), (0, 1), (0, 0))
        for along_core in (1, 0)
    ][:-1]

    def step_from(sign, step):
        along_x, along_y, along_core = step
        return (
            4 * lax.rem(x + 4 + sign * along_x, 4)
            + 2 * lax.rem(y + along_y, 2)
            + lax.rem(core + along_core, 2)
        )

    def to_group(src, dst, phase, sign, by_slot):
        for k, step in enumerate(steps, 1):
            peer = step_from(sign, step)
            pltpu.make_async_remote_copy(
                src_ref=src.at[k if by_slot else peer],
                dst_ref=dst.at[k],
                send_sem=send_sem.at[phase],
                recv_sem=recv_sem.at[phase],
                device_id={"group": peer, "tensor": t},
                device_id_type=MESH,
            ).start()

    to_group(send_a, recv_a, 0, 1, False)
    recv_a[0] = send_a[g]

    def put(src, dst, other, phase):
        @pl.when(jnp.logical_not(same(other)))
        def _():
            pltpu.make_async_remote_copy(
                src_ref=src,
                dst_ref=dst,
                send_sem=send_sem.at[phase],
                recv_sem=recv_sem.at[phase],
                device_id=other,
                device_id_type=MESH,
            ).start()

        @pl.when(same(other))
        def _():
            pltpu.make_async_copy(src, dst, recv_sem.at[phase]).start()

    for layer in range(LAYERS):
        for j in range(2):
            longs[layer][j].start()
            shorts[layer][j].start()
    late.start()
    far_barrier()
    put(new_kv.at[1, pl.ds(0,256)], new_1.at[pl.ds(0,256)], there, 4)

    row = lax.broadcasted_iota(jnp.int32, (QPK * ROWS, 1), 0)
    row_seq = lax.rem(row, SEQS)

    def stale(layer):
        every = stack_rows(q_v[:, layer])
        q = jnp.concatenate([every[:, i * HD : (i + 1) * HD] for i in range(QPK)], axis=0)
        q16 = q.astype(BF16)
        scores = []
        blocks = []
        for j in range(2):
            longs[layer][j].wait()
            shorts[layer][j].wait()
            for held, seq in ((long_v, 2 * j), (short_v, 2 * j + 1)):
                s = lax.dot_general(
                    q16, held[layer, j, :, :HD], (((1,), (1,)), ((), ())), preferred_element_type=F32
                )
                col = lax.broadcasted_iota(jnp.int32, s.shape, 1)
                keep = (col < lengths[seq]) & (row_seq == seq)
                scores.append(jnp.where(keep, s * UNIT, FAR))
                blocks.append((held, j))
        top = functools.reduce(
            jnp.maximum, [jnp.max(s, axis=1, keepdims=True) for s in scores]
        )
        total = jnp.zeros_like(top)
        mixed = jnp.zeros((QPK * ROWS, HD), F32)
        for s, (held, j) in zip(scores, blocks):
            weight = jnp.exp2(s - top)
            total = total + jnp.sum(weight, axis=1, keepdims=True)
            mixed = mixed + jnp.dot(weight.astype(BF16), held[layer, j, :, HD:], preferred_element_type=F32)
        shape = (QPK, ROWS)
        return (
            q.reshape(*shape, HD),
            top.reshape(*shape, 1),
            total.reshape(*shape, 1),
            mixed.reshape(*shape, HD),
        )

    upper = lax.broadcasted_iota(jnp.int32, (ROWS, HD), 0) < SEQS

    def by_step(fresh):
        other = jnp.concatenate([fresh[SEQS:], fresh[:SEQS]], axis=0)
        return jnp.where(upper, fresh, other), jnp.where(upper, other, fresh)

    def merge(key, value, part):
        q, top, total, mixed = part
        key_0, key_1 = by_step(key.astype(BF16).astype(F32))
        value_0, value_1 = by_step(value.astype(BF16).astype(F32))
        s_0 = jnp.sum(q * key_0[None], axis=2, keepdims=True) * UNIT
        s_1 = jnp.sum(q * key_1[None], axis=2, keepdims=True) * UNIT
        s_1 = jnp.where(upper[None, :, :1], FAR, s_1)
        peak = jnp.maximum(top, jnp.maximum(s_0, s_1))
        keep = jnp.exp2(top - peak)
        w_0 = jnp.exp2(s_0 - peak)
        w_1 = jnp.exp2(s_1 - peak)
        norm = 1.0 / (total * keep + w_0 + w_1)
        result = (mixed * keep + w_0 * value_0[None] + w_1 * value_1[None]) * norm
        return result.astype(BF16).astype(F32)

    def fold(products):
        products = products.reshape(groups, ROWS, 2 * HD)
        return jnp.concatenate([products[:, :, :HD], products[:, :, HD:]], axis=1).astype(BF16)

    def flatten(features):
        return jnp.concatenate(
            [features[:, :ROWS].reshape(-1, half), features[:, ROWS:].reshape(-1, half)], axis=1
        ).astype(BF16)

    for copy in loads[1:]:
        copy.wait()

    rest = pl.ds(1, groups - 1)
    whole(recv_a.at[rest], recv_sem.at[0]).wait()
    flat = flatten(recv_a[...].astype(F32))
    by_new = jnp.dot(flat, new_0[...], preferred_element_type=F32)
    by_old = jnp.dot(flat, old_0[...], preferred_element_type=F32)
    row_step = lax.rem(lax.broadcasted_iota(jnp.int32, by_new.shape, 0), ROWS) // SEQS
    send_b[...] = fold(jnp.where(row_step >= switch[0], by_new, by_old))
    to_group(send_b, recv_b, 1, -1, True)
    put(new_kv.at[1, pl.ds(256,256)], new_1.at[pl.ds(256,256)], there, 4)
    recv_b[0] = send_b[0]
    part_0 = stale(0)

    own = stack_rows(own_v[...])
    whole(recv_b.at[rest], recv_sem.at[1]).wait()
    summed = jnp.sum(recv_b[...].astype(F32), axis=0)
    attended_0 = merge(summed[:ROWS] * scale_0, summed[ROWS:] * scale_0, part_0)
    hidden = [own[:, i * HD : (i + 1) * HD] + attended_0[i] for i in range(QPK)]
    for h in range(2):
        send_c[h] = jnp.concatenate(
            [jnp.concatenate(hidden[4 * h + 2 * r : 4 * h + 2 * r + 2], axis=1) for r in range(2)],
            axis=0,
        ).astype(BF16)

    for step in steps:
        peer = step_from(1, step)
        pltpu.make_async_remote_copy(
            src_ref=send_c.at[lax.rem(core + step[2], 2)],
            dst_ref=recv_c.at[g],
            send_sem=send_sem.at[2],
            recv_sem=recv_sem.at[2],
            device_id=device(peer, t),
            device_id_type=MESH,
        ).start()
    pltpu.make_async_copy(send_c.at[core], recv_c.at[g], recv_sem.at[2]).start()
    for k in range(1, tensors):
        pltpu.make_async_remote_copy(
            src_ref=send_c,
            dst_ref=recv_t.at[t],
            send_sem=send_sem.at[5],
            recv_sem=recv_sem.at[5],
            device_id=device(g, lax.rem(t + k, tensors)),
            device_id_type=MESH,
        ).start()
    pltpu.make_async_copy(send_c, recv_t.at[t], recv_sem.at[5]).start()

    part_1 = stale(1)
    whole(new_1, recv_sem.at[4]).wait()
    whole(recv_c, recv_sem.at[2]).wait()
    flat = flatten(recv_c[...].astype(F32))
    send_d[...] = fold(jnp.dot(flat, new_1[...], preferred_element_type=F32))
    for peer in (1, 0, 3, 2, 13, 12, 5, 4, 15, 14, 7, 6, 9, 8, 11, 10):
        put(send_d.at[peer], recv_d.at[2 * t + core], device(peer, column), 3)

    late.wait()
    whole(recv_t, recv_sem.at[5]).wait()
    parts = [recv_t[i, h].astype(F32) for i in range(tensors) for h in range(2)]
    wide = jnp.concatenate([part[at : at + ROWS] for part in parts for at in (0, ROWS)], axis=1)
    scale_1 = lax.rsqrt(jnp.sum(wide * wide, axis=1, keepdims=True) / width + 1e-05)
    by_old = jnp.dot(wide.astype(BF16), old_1[...], preferred_element_type=F32)
    use_new = lax.broadcasted_iota(jnp.int32, (ROWS, HD), 0) // SEQS >= switch[1]

    whole(recv_d, recv_sem.at[3]).wait()
    summed = jnp.sum(recv_d[...].astype(F32), axis=0)
    key = jnp.where(use_new, summed[:ROWS], by_old[:, :HD]) * scale_1
    value = jnp.where(use_new, summed[ROWS:], by_old[:, HD:]) * scale_1
    attended_1 = merge(key, value, part_1)
    for i in range(QPK):
        rows = (hidden[i] + attended_1[i]).astype(BF16)
        out[0, :, i * HD : (i + 1) * HD] = rows[:SEQS]
        out[1, :, i * HD : (i + 1) * HD] = rows[SEQS:]

    for phase, src in ((0, send_a), (1, send_b), (2, recv_c)):
        whole(src.at[rest], send_sem.at[phase]).wait()
    whole(recv_t.at[pl.ds(1, tensors - 1)], send_sem.at[5]).wait()

    @pl.when(jnp.logical_not(same(there)))
    def _():
        whole(new_1, send_sem.at[4]).wait()

    @pl.when(column != t)
    def _():
        whole(send_d, send_sem.at[3]).wait()

    @pl.when(column == t)
    def _():
        whole(send_d.at[rest], send_sem.at[3]).wait()


def solution(mesh):
    groups, tensors = mesh.shape["group"], mesh.shape["tensor"]

    def per_device(*operands):
        tokens, queries, cache_kv, old_kv, new_kv, switch, lengths = operands
        depth = new_kv.shape[1]
        half = depth // 2
        block = tokens.shape[2] // tensors
        cache_len = cache_kv.shape[2]
        hbm = pl.BlockSpec(memory_space=pltpu.HBM)
        vmem = pltpu.VMEM
        result = pl.pallas_call(
            functools.partial(kernel, groups, tensors),
            out_shape=jax.ShapeDtypeStruct((STEPS, SEQS, block), BF16),
            in_specs=[hbm] * 7,
            out_specs=pl.BlockSpec(memory_space=vmem),
            scratch_shapes=[
                pltpu.SMEM(switch.shape, jnp.int32),
                pltpu.SMEM(lengths.shape, jnp.int32),
                vmem(tokens.shape, BF16),
                vmem((STEPS, SEQS, block), BF16),
                vmem(queries.shape, BF16),
                vmem((LAYERS, 2, cache_len, 2 * HD), BF16),
                vmem((LAYERS, 2, SHORT, 2 * HD), BF16),
                vmem((depth, 2 * HD), BF16),
                vmem(old_kv.shape[1:], BF16),
                vmem((depth, 2 * HD), BF16),
                vmem((depth, 2 * HD), BF16),
                vmem((groups, 2 * ROWS, half), BF16),
                vmem((groups, 2 * ROWS, half), BF16),
                vmem((groups, 2 * ROWS, HD), BF16),
                vmem((groups, 2 * ROWS, HD), BF16),
                vmem((2, 2 * ROWS, half), BF16),
                vmem((groups, 2 * ROWS, half), BF16),
                vmem((tensors, 2, 2 * ROWS, half), BF16),
                vmem((groups, 2 * ROWS, HD), BF16),
                vmem((groups, 2 * ROWS, HD), BF16),
                pltpu.SemaphoreType.DMA((8,)),
                pltpu.SemaphoreType.DMA((LAYERS, 2)),
                pltpu.SemaphoreType.DMA((LAYERS, 2)),
                pltpu.SemaphoreType.DMA((6,)),
                pltpu.SemaphoreType.DMA((6,)),
                pltpu.SemaphoreType.REGULAR,
                pltpu.SemaphoreType.REGULAR,
            ],
            compiler_params=pltpu.CompilerParams(
                collective_id=0, has_side_effects=True, vmem_limit_bytes=40 * 2**20
            ),
        )(*[pltpu.with_memory_space_constraint(operand, pltpu.HBM) for operand in operands])
        return result

    return jax.shard_map(
        per_device,
        mesh=mesh,
        in_specs=(
            P(None, "group", None),
            P(None, None, "group", "tensor"),
            P(None, "group", None, "tensor"),
            P(None, None, "tensor"),
            P(None, "group", "tensor"),
            P(),
            P("group"),
        ),
        out_specs=P(None, "group", "tensor"),
        check_vma=False,
    )
```

```python
import functools
import math

import jax
import jax.numpy as jnp
from jax import lax
from jax.experimental import pallas as pl
from jax.experimental.pallas import tpu as pltpu
from jax.sharding import PartitionSpec as P

MESH = pl.DeviceIdType.MESH
F32, BF16 = jnp.float32, jnp.bfloat16
HD = 128
QPK = 8
LAYERS = 2
STEPS = 2
SEQS = 4
ROWS = STEPS * SEQS
SHORT = 16
FAR = -1e30
UNIT = HD**-0.5 * math.log2(math.e)


def stack_rows(ref_value):
    wide = ref_value.astype(F32)
    return jnp.concatenate([wide[0], wide[1]], axis=0)


def kernel(
    groups,
    tensors,
    tokens,
    queries,
    cache,
    old_kv,
    new_kv,
    switch_hbm,
    lengths_hbm,
    out,
    switch,
    lengths,
    tok_v,
    own_v,
    q_v,
    long_v,
    short_v,
    old_0,
    old_1,
    new_0,
    new_1,
    send_a,
    recv_a,
    send_b,
    recv_b,
    send_c,
    recv_c,
    recv_t,
    send_d,
    recv_d,
    load_sem,
    long_sem,
    short_sem,
    send_sem,
    recv_sem,
    near_sem,
    far_sem,
):
    g = lax.axis_index("group")
    t = lax.axis_index("tensor")
    depth = new_kv.shape[1]
    half = depth // 2
    width = tokens.shape[2]
    block = width // tensors
    x, y, core = g // 4, lax.rem(g // 2, 2), lax.rem(g, 2)

    def device(group, tensor):
        return {"group": group, "tensor": tensor}

    def holder(row_block, column_block):
        across = lax.rem(row_block // 4 + column_block + 1, 4)
        along = lax.rem(row_block // 2 + column_block // 4 + column_block, 2)
        return 4 * across + 2 * along + lax.rem(row_block, 2)

    def route(side):
        goes = device(holder(2 * (g // 2) + side, t), g // 2)
        low = lax.rem(x + 7 - t // 2, 4)
        return goes, 4 * lax.rem(y + t + low, 2) + low

    def targets(side):
        goes, columns = route(side)
        yield goes
        for group in range(groups):
            yield device(group, columns)

    there, column = route(core)
    origin = device(2 * t + core, column)

    def same(other):
        return (other["group"] == g) & (other["tensor"] == t)

    barrier = pltpu.get_barrier_semaphore()
    mate = device(g + 1 - 2 * core, t)

    def greet(other):
        pl.semaphore_signal(barrier, inc=1, device_id=other, device_id_type=MESH)

    def same_chip(other):
        return (other["group"] // 2 == g // 2) & (other["tensor"] == t)

    def senders():
        yield origin
        for block_index in range(groups):
            yield device(holder(block_index, t), block_index // 2)

    for k in range(1, groups // 2):
        greet(device(2 * lax.rem(g // 2 + k, groups // 2), t))

    @pl.when(core == 1)
    def _():
        greet(mate)

    load_tokens = pltpu.make_async_copy(tokens, tok_v, load_sem.at[0])
    load_tokens.start()

    for k in range(1, tensors):
        greet(device(g - core + 1, lax.rem(t + k, tensors)))
    for other in senders():

        @pl.when(jnp.logical_not(same_chip(other)))
        def _():
            greet(device(2 * (other["group"] // 2) + 1, other["tensor"]))

    loads = [
        load_tokens,
        pltpu.make_async_copy(
            tokens.at[:, :, pl.ds(pl.multiple_of(t * block, block), block)],
            own_v,
            load_sem.at[1],
        ),
        pltpu.make_async_copy(queries, q_v, load_sem.at[2]),
        pltpu.make_async_copy(new_kv.at[0], new_0, load_sem.at[3]),
        pltpu.make_async_copy(
            old_kv.at[0, pl.ds(pl.multiple_of(g * depth, depth), depth), :],
            old_0,
            load_sem.at[4],
        ),
        pltpu.make_async_copy(switch_hbm, switch, load_sem.at[5]),
        pltpu.make_async_copy(lengths_hbm, lengths, load_sem.at[6]),
    ]
    late = pltpu.make_async_copy(old_kv.at[1], old_1, load_sem.at[7])
    longs = [
        [
            pltpu.make_async_copy(
                cache.at[layer, 2 * j], long_v.at[layer, j], long_sem.at[layer, j]
            )
            for j in range(2)
        ]
        for layer in range(LAYERS)
    ]
    shorts = [
        [
            pltpu.make_async_copy(
                cache.at[layer, 2 * j + 1, pl.ds(0, SHORT)],
                short_v.at[layer, j],
                short_sem.at[layer, j],
            )
            for j in range(2)
        ]
        for layer in range(LAYERS)
    ]
    for copy in loads[1:]:
        copy.start()

    loads[0].wait()
    mine = stack_rows(tok_v[...])
    for k in range(groups):
        piece = mine[:, k * depth : (k + 1) * depth]
        send_a[k] = jnp.concatenate([piece[:, :half], piece[:, half:]], axis=0).astype(BF16)
    scale_0 = lax.rsqrt(jnp.sum(mine * mine, axis=1, keepdims=True) / width + 1e-05)

    @pl.when(core == 0)
    def _():
        pl.semaphore_wait(barrier, groups - 1)
        pl.semaphore_signal(near_sem, inc=1, device_id=mate, device_id_type=MESH)

    @pl.when(core == 1)
    def _():
        pl.semaphore_wait(near_sem, 1)

    def far_barrier():
        count = 2 * (tensors - 1)
        for other_core in range(2):
            for other in targets(other_core):
                count = count + jnp.logical_not(same_chip(other)).astype(jnp.int32)

        @pl.when(core == 1)
        def _():
            pl.semaphore_wait(barrier, count)
            pl.semaphore_signal(far_sem, inc=1, device_id=mate, device_id_type=MESH)

        @pl.when(core == 0)
        def _():
            pl.semaphore_wait(far_sem, 1)

    def whole(ref, sem):
        return pltpu.make_async_copy(ref, ref, sem)

    steps = [
        (along_x, along_y, along_core)
        for along_x, along_y in ((2, 1), (1, 1), (3, 1), (2, 0), (1, 0), (3, 0), (0, 1), (0, 0))
        for along_core in (1, 0)
    ][:-1]

    def step_from(sign, step):
        along_x, along_y, along_core = step
        return (
            4 * lax.rem(x + 4 + sign * along_x, 4)
            + 2 * lax.rem(y + along_y, 2)
            + lax.rem(core + along_core, 2)
        )

    def to_group(src, dst, phase, sign, by_slot):
        for k, step in enumerate(steps, 1):
            peer = step_from(sign, step)
            pltpu.make_async_remote_copy(
                src_ref=src.at[k if by_slot else peer],
                dst_ref=dst.at[k],
                send_sem=send_sem.at[phase],
                recv_sem=recv_sem.at[phase],
                device_id={"group": peer, "tensor": t},
                device_id_type=MESH,
            ).start()

    to_group(send_a, recv_a, 0, 1, False)
    recv_a[0] = send_a[g]

    def put(src, dst, other, phase):
        @pl.when(jnp.logical_not(same(other)))
        def _():
            pltpu.make_async_remote_copy(
                src_ref=src,
                dst_ref=dst,
                send_sem=send_sem.at[phase],
                recv_sem=recv_sem.at[phase],
                device_id=other,
                device_id_type=MESH,
            ).start()

        @pl.when(same(other))
        def _():
            pltpu.make_async_copy(src, dst, recv_sem.at[phase]).start()

    for layer in range(LAYERS):
        for j in range(2):
            longs[layer][j].start()
            shorts[layer][j].start()
    late.start()
    def move(piece):
        rows = pl.ds(piece * (depth // 4), depth // 4)
        put(new_kv.at[1, rows], new_1.at[rows], there, 4)

    far_barrier()
    move(0)

    row = lax.broadcasted_iota(jnp.int32, (QPK * ROWS, 1), 0)
    row_seq = lax.rem(row, SEQS)

    def stale(layer):
        every = stack_rows(q_v[:, layer])
        q = jnp.concatenate([every[:, i * HD : (i + 1) * HD] for i in range(QPK)], axis=0)
        q16 = q.astype(BF16)
        scores = []
        blocks = []
        for j in range(2):
            longs[layer][j].wait()
            shorts[layer][j].wait()
            for held, seq in ((long_v, 2 * j), (short_v, 2 * j + 1)):
                s = lax.dot_general(
                    q16, held[layer, j, :, :HD], (((1,), (1,)), ((), ())), preferred_element_type=F32
                )
                col = lax.broadcasted_iota(jnp.int32, s.shape, 1)
                keep = (col < lengths[seq]) & (row_seq == seq)
                scores.append(jnp.where(keep, s * UNIT, FAR))
                blocks.append((held, j))
        top = functools.reduce(
            jnp.maximum, [jnp.max(s, axis=1, keepdims=True) for s in scores]
        )
        total = jnp.zeros_like(top)
        mixed = jnp.zeros((QPK * ROWS, HD), F32)
        for s, (held, j) in zip(scores, blocks):
            weight = jnp.exp2(s - top)
            total = total + jnp.sum(weight, axis=1, keepdims=True)
            mixed = mixed + jnp.dot(weight.astype(BF16), held[layer, j, :, HD:], preferred_element_type=F32)
        shape = (QPK, ROWS)
        return (
            q.reshape(*shape, HD),
            top.reshape(*shape, 1),
            total.reshape(*shape, 1),
            mixed.reshape(*shape, HD),
        )

    upper = lax.broadcasted_iota(jnp.int32, (ROWS, HD), 0) < SEQS

    def by_step(fresh):
        other = jnp.concatenate([fresh[SEQS:], fresh[:SEQS]], axis=0)
        return jnp.where(upper, fresh, other), jnp.where(upper, other, fresh)

    def merge(key, value, part):
        q, top, total, mixed = part
        key_0, key_1 = by_step(key.astype(BF16).astype(F32))
        value_0, value_1 = by_step(value.astype(BF16).astype(F32))
        s_0 = jnp.sum(q * key_0[None], axis=2, keepdims=True) * UNIT
        s_1 = jnp.sum(q * key_1[None], axis=2, keepdims=True) * UNIT
        s_1 = jnp.where(upper[None, :, :1], FAR, s_1)
        peak = jnp.maximum(top, jnp.maximum(s_0, s_1))
        keep = jnp.exp2(top - peak)
        w_0 = jnp.exp2(s_0 - peak)
        w_1 = jnp.exp2(s_1 - peak)
        norm = 1.0 / (total * keep + w_0 + w_1)
        result = (mixed * keep + w_0 * value_0[None] + w_1 * value_1[None]) * norm
        return result.astype(BF16).astype(F32)

    def fold(products):
        products = products.reshape(groups, ROWS, 2 * HD)
        return jnp.concatenate([products[:, :, :HD], products[:, :, HD:]], axis=1).astype(BF16)

    def flatten(features):
        return jnp.concatenate(
            [features[:, :ROWS].reshape(-1, half), features[:, ROWS:].reshape(-1, half)], axis=1
        ).astype(BF16)

    for copy in loads[1:]:
        copy.wait()

    rest = pl.ds(1, groups - 1)
    part_0 = stale(0)
    move(1)
    whole(recv_a.at[rest], recv_sem.at[0]).wait()
    flat = flatten(recv_a[...].astype(F32))
    by_new = jnp.dot(flat, new_0[...], preferred_element_type=F32)
    by_old = jnp.dot(flat, old_0[...], preferred_element_type=F32)
    row_step = lax.rem(lax.broadcasted_iota(jnp.int32, by_new.shape, 0), ROWS) // SEQS
    send_b[...] = fold(jnp.where(row_step >= switch[0], by_new, by_old))
    to_group(send_b, recv_b, 1, -1, True)
    move(2)
    part_1 = stale(1)
    move(3)
    recv_b[0] = send_b[0]

    own = stack_rows(own_v[...])
    whole(recv_b.at[rest], recv_sem.at[1]).wait()
    summed = jnp.sum(recv_b[...].astype(F32), axis=0)
    attended_0 = merge(summed[:ROWS] * scale_0, summed[ROWS:] * scale_0, part_0)
    hidden = [own[:, i * HD : (i + 1) * HD] + attended_0[i] for i in range(QPK)]
    for h in range(2):
        send_c[h] = jnp.concatenate(
            [jnp.concatenate(hidden[4 * h + 2 * r : 4 * h + 2 * r + 2], axis=1) for r in range(2)],
            axis=0,
        ).astype(BF16)

    for step in steps:
        peer = step_from(1, step)
        pltpu.make_async_remote_copy(
            src_ref=send_c.at[lax.rem(core + step[2], 2)],
            dst_ref=recv_c.at[g],
            send_sem=send_sem.at[2],
            recv_sem=recv_sem.at[2],
            device_id=device(peer, t),
            device_id_type=MESH,
        ).start()
    pltpu.make_async_copy(send_c.at[core], recv_c.at[g], recv_sem.at[2]).start()
    for k in range(1, tensors):
        pltpu.make_async_remote_copy(
            src_ref=send_c,
            dst_ref=recv_t.at[t],
            send_sem=send_sem.at[5],
            recv_sem=recv_sem.at[5],
            device_id=device(g, lax.rem(t + k, tensors)),
            device_id_type=MESH,
        ).start()
    pltpu.make_async_copy(send_c, recv_t.at[t], recv_sem.at[5]).start()

    whole(new_1, recv_sem.at[4]).wait()
    whole(recv_c, recv_sem.at[2]).wait()
    flat = flatten(recv_c[...].astype(F32))
    send_d[...] = fold(jnp.dot(flat, new_1[...], preferred_element_type=F32))
    for peer in (1, 0, 3, 2, 13, 12, 5, 4, 15, 14, 7, 6, 9, 8, 11, 10):
        put(send_d.at[peer], recv_d.at[2 * t + core], device(peer, column), 3)

    late.wait()
    whole(recv_t, recv_sem.at[5]).wait()
    parts = [recv_t[i, h].astype(F32) for i in range(tensors) for h in range(2)]
    wide = jnp.concatenate([part[at : at + ROWS] for part in parts for at in (0, ROWS)], axis=1)
    scale_1 = lax.rsqrt(jnp.sum(wide * wide, axis=1, keepdims=True) / width + 1e-05)
    by_old = jnp.dot(wide.astype(BF16), old_1[...], preferred_element_type=F32)
    use_new = lax.broadcasted_iota(jnp.int32, (ROWS, HD), 0) // SEQS >= switch[1]

    whole(recv_d, recv_sem.at[3]).wait()
    summed = jnp.sum(recv_d[...].astype(F32), axis=0)
    key = jnp.where(use_new, summed[:ROWS], by_old[:, :HD]) * scale_1
    value = jnp.where(use_new, summed[ROWS:], by_old[:, HD:]) * scale_1
    attended_1 = merge(key, value, part_1)
    for i in range(QPK):
        rows = (hidden[i] + attended_1[i]).astype(BF16)
        out[0, :, i * HD : (i + 1) * HD] = rows[:SEQS]
        out[1, :, i * HD : (i + 1) * HD] = rows[SEQS:]

    for phase, src in ((0, send_a), (1, send_b), (2, recv_c)):
        whole(src.at[rest], send_sem.at[phase]).wait()
    whole(recv_t.at[pl.ds(1, tensors - 1)], send_sem.at[5]).wait()

    @pl.when(jnp.logical_not(same(there)))
    def _():
        whole(new_1, send_sem.at[4]).wait()

    @pl.when(column != t)
    def _():
        whole(send_d, send_sem.at[3]).wait()

    @pl.when(column == t)
    def _():
        whole(send_d.at[rest], send_sem.at[3]).wait()


def solution(mesh):
    groups, tensors = mesh.shape["group"], mesh.shape["tensor"]

    def per_device(*operands):
        tokens, queries, cache_kv, old_kv, new_kv, switch, lengths = operands
        depth = new_kv.shape[1]
        half = depth // 2
        block = tokens.shape[2] // tensors
        cache_len = cache_kv.shape[2]
        hbm = pl.BlockSpec(memory_space=pltpu.HBM)
        vmem = pltpu.VMEM
        result = pl.pallas_call(
            functools.partial(kernel, groups, tensors),
            out_shape=jax.ShapeDtypeStruct((STEPS, SEQS, block), BF16),
            in_specs=[hbm] * 7,
            out_specs=pl.BlockSpec(memory_space=vmem),
            scratch_shapes=[
                pltpu.SMEM(switch.shape, jnp.int32),
                pltpu.SMEM(lengths.shape, jnp.int32),
                vmem(tokens.shape, BF16),
                vmem((STEPS, SEQS, block), BF16),
                vmem(queries.shape, BF16),
                vmem((LAYERS, 2, cache_len, 2 * HD), BF16),
                vmem((LAYERS, 2, SHORT, 2 * HD), BF16),
                vmem((depth, 2 * HD), BF16),
                vmem(old_kv.shape[1:], BF16),
                vmem((depth, 2 * HD), BF16),
                vmem((depth, 2 * HD), BF16),
                vmem((groups, 2 * ROWS, half), BF16),
                vmem((groups, 2 * ROWS, half), BF16),
                vmem((groups, 2 * ROWS, HD), BF16),
                vmem((groups, 2 * ROWS, HD), BF16),
                vmem((2, 2 * ROWS, half), BF16),
                vmem((groups, 2 * ROWS, half), BF16),
                vmem((tensors, 2, 2 * ROWS, half), BF16),
                vmem((groups, 2 * ROWS, HD), BF16),
                vmem((groups, 2 * ROWS, HD), BF16),
                pltpu.SemaphoreType.DMA((8,)),
                pltpu.SemaphoreType.DMA((LAYERS, 2)),
                pltpu.SemaphoreType.DMA((LAYERS, 2)),
                pltpu.SemaphoreType.DMA((6,)),
                pltpu.SemaphoreType.DMA((6,)),
                pltpu.SemaphoreType.REGULAR,
                pltpu.SemaphoreType.REGULAR,
            ],
            compiler_params=pltpu.CompilerParams(
                collective_id=0, has_side_effects=True, vmem_limit_bytes=40 * 2**20
            ),
        )(*[pltpu.with_memory_space_constraint(operand, pltpu.HBM) for operand in operands])
        return result

    return jax.shard_map(
        per_device,
        mesh=mesh,
        in_specs=(
            P(None, "group", None),
            P(None, None, "group", "tensor"),
            P(None, "group", None, "tensor"),
            P(None, None, "tensor"),
            P(None, "group", "tensor"),
            P(),
            P("group"),
        ),
        out_specs=P(None, "group", "tensor"),
        check_vma=False,
    )
```

```python
import functools
import math

import jax
import jax.numpy as jnp
from jax import lax
from jax.experimental import pallas as pl
from jax.experimental.pallas import tpu as pltpu
from jax.sharding import PartitionSpec as P

MESH = pl.DeviceIdType.MESH
F32, BF16 = jnp.float32, jnp.bfloat16
HD = 128
QPK = 8
LAYERS = 2
STEPS = 2
SEQS = 4
ROWS = STEPS * SEQS
SHORT = 16
FAR = -1e30
UNIT = HD**-0.5 * math.log2(math.e)


def stack_rows(ref_value):
    wide = ref_value.astype(F32)
    return jnp.concatenate([wide[0], wide[1]], axis=0)


def kernel(
    groups,
    tensors,
    tokens,
    queries,
    cache,
    old_kv,
    new_kv,
    switch_hbm,
    lengths_hbm,
    out,
    switch,
    lengths,
    tok_v,
    own_v,
    q_v,
    long_v,
    short_v,
    old_0,
    old_1,
    new_0,
    new_1,
    send_a,
    recv_a,
    send_b,
    recv_b,
    send_c,
    recv_c,
    recv_t,
    send_d,
    recv_d,
    load_sem,
    long_sem,
    short_sem,
    send_sem,
    recv_sem,
    near_sem,
    far_sem,
):
    g = lax.axis_index("group")
    t = lax.axis_index("tensor")
    depth = new_kv.shape[1]
    half = depth // 2
    width = tokens.shape[2]
    block = width // tensors
    x, y, core = g // 4, lax.rem(g // 2, 2), lax.rem(g, 2)

    def device(group, tensor):
        return {"group": group, "tensor": tensor}

    def holder(row_block, column_block):
        across = lax.rem(row_block // 4 + column_block + 1, 4)
        along = lax.rem(row_block // 2 + column_block // 4 + column_block, 2)
        return 4 * across + 2 * along + lax.rem(row_block, 2)

    def route(side):
        goes = device(holder(2 * (g // 2) + side, t), g // 2)
        low = lax.rem(x + 7 - t // 2, 4)
        return goes, 4 * lax.rem(y + t + low, 2) + low

    def targets(side):
        goes, columns = route(side)
        yield goes
        for group in range(groups):
            yield device(group, columns)

    there, column = route(core)
    origin = device(2 * t + core, column)

    def same(other):
        return (other["group"] == g) & (other["tensor"] == t)

    barrier = pltpu.get_barrier_semaphore()
    mate = device(g + 1 - 2 * core, t)

    def greet(other):
        pl.semaphore_signal(barrier, inc=1, device_id=other, device_id_type=MESH)

    def same_chip(other):
        return (other["group"] // 2 == g // 2) & (other["tensor"] == t)

    def senders():
        yield origin
        for block_index in range(groups):
            yield device(holder(block_index, t), block_index // 2)

    for k in range(1, groups // 2):
        greet(device(2 * lax.rem(g // 2 + k, groups // 2), t))

    @pl.when(core == 1)
    def _():
        greet(mate)

    load_tokens = pltpu.make_async_copy(tokens, tok_v, load_sem.at[0])
    load_tokens.start()

    for k in range(1, tensors):
        greet(device(g - core + 1, lax.rem(t + k, tensors)))
    for other in senders():

        @pl.when(jnp.logical_not(same_chip(other)))
        def _():
            greet(device(2 * (other["group"] // 2) + 1, other["tensor"]))

    loads = [
        load_tokens,
        pltpu.make_async_copy(
            tokens.at[:, :, pl.ds(pl.multiple_of(t * block, block), block)],
            own_v,
            load_sem.at[1],
        ),
        pltpu.make_async_copy(queries, q_v, load_sem.at[2]),
        pltpu.make_async_copy(new_kv.at[0], new_0, load_sem.at[3]),
        pltpu.make_async_copy(
            old_kv.at[0, pl.ds(pl.multiple_of(g * depth, depth), depth), :],
            old_0,
            load_sem.at[4],
        ),
        pltpu.make_async_copy(switch_hbm, switch, load_sem.at[5]),
        pltpu.make_async_copy(lengths_hbm, lengths, load_sem.at[6]),
    ]
    late = pltpu.make_async_copy(old_kv.at[1], old_1, load_sem.at[7])
    longs = [
        [
            pltpu.make_async_copy(
                cache.at[layer, 2 * j], long_v.at[layer, j], long_sem.at[layer, j]
            )
            for j in range(2)
        ]
        for layer in range(LAYERS)
    ]
    shorts = [
        [
            pltpu.make_async_copy(
                cache.at[layer, 2 * j + 1, pl.ds(0, SHORT)],
                short_v.at[layer, j],
                short_sem.at[layer, j],
            )
            for j in range(2)
        ]
        for layer in range(LAYERS)
    ]
    for copy in loads[1:]:
        copy.start()

    loads[0].wait()
    mine = stack_rows(tok_v[...])
    for k in range(groups):
        piece = mine[:, k * depth : (k + 1) * depth]
        send_a[k] = jnp.concatenate([piece[:, :half], piece[:, half:]], axis=0).astype(BF16)
    scale_0 = lax.rsqrt(jnp.sum(mine * mine, axis=1, keepdims=True) / width + 1e-05)

    @pl.when(core == 0)
    def _():
        pl.semaphore_wait(barrier, groups - 1)
        pl.semaphore_signal(near_sem, inc=1, device_id=mate, device_id_type=MESH)

    @pl.when(core == 1)
    def _():
        pl.semaphore_wait(near_sem, 1)

    def far_barrier():
        count = 2 * (tensors - 1)
        for other_core in range(2):
            for other in targets(other_core):
                count = count + jnp.logical_not(same_chip(other)).astype(jnp.int32)

        @pl.when(core == 1)
        def _():
            pl.semaphore_wait(barrier, count)
            pl.semaphore_signal(far_sem, inc=1, device_id=mate, device_id_type=MESH)

        @pl.when(core == 0)
        def _():
            pl.semaphore_wait(far_sem, 1)

    def whole(ref, sem):
        return pltpu.make_async_copy(ref, ref, sem)

    steps = [
        (along_x, along_y, along_core)
        for along_x, along_y in ((2, 1), (1, 1), (3, 1), (2, 0), (1, 0), (3, 0), (0, 1), (0, 0))
        for along_core in (0, 1)
        if along_x or along_y or along_core
    ]

    def step_from(sign, step):
        along_x, along_y, along_core = step
        return (
            4 * lax.rem(x + 4 + sign * along_x, 4)
            + 2 * lax.rem(y + along_y, 2)
            + lax.rem(core + along_core, 2)
        )

    def to_group(src, dst, phase, sign, by_slot):
        for k, step in enumerate(steps, 1):
            peer = step_from(sign, step)
            pltpu.make_async_remote_copy(
                src_ref=src.at[k if by_slot else peer],
                dst_ref=dst.at[k],
                send_sem=send_sem.at[phase],
                recv_sem=recv_sem.at[phase],
                device_id={"group": peer, "tensor": t},
                device_id_type=MESH,
            ).start()

    to_group(send_a, recv_a, 0, 1, False)
    recv_a[0] = send_a[g]

    def put(src, dst, other, phase):
        @pl.when(jnp.logical_not(same(other)))
        def _():
            pltpu.make_async_remote_copy(
                src_ref=src,
                dst_ref=dst,
                send_sem=send_sem.at[phase],
                recv_sem=recv_sem.at[phase],
                device_id=other,
                device_id_type=MESH,
            ).start()

        @pl.when(same(other))
        def _():
            pltpu.make_async_copy(src, dst, recv_sem.at[phase]).start()

    for layer in range(LAYERS):
        for j in range(2):
            longs[layer][j].start()
            shorts[layer][j].start()
    late.start()
    def move(piece):
        rows = pl.ds(piece * (depth // 4), depth // 4)
        put(new_kv.at[1, rows], new_1.at[rows], there, 4)

    far_barrier()
    move(0)

    row = lax.broadcasted_iota(jnp.int32, (QPK * ROWS, 1), 0)
    row_seq = lax.rem(row, SEQS)

    def stale(layer):
        every = stack_rows(q_v[:, layer])
        q = jnp.concatenate([every[:, i * HD : (i + 1) * HD] for i in range(QPK)], axis=0)
        q16 = q.astype(BF16)
        scores = []
        blocks = []
        for j in range(2):
            longs[layer][j].wait()
            shorts[layer][j].wait()
            for held, seq in ((long_v, 2 * j), (short_v, 2 * j + 1)):
                s = lax.dot_general(
                    q16, held[layer, j, :, :HD], (((1,), (1,)), ((), ())), preferred_element_type=F32
                )
                col = lax.broadcasted_iota(jnp.int32, s.shape, 1)
                keep = (col < lengths[seq]) & (row_seq == seq)
                scores.append(jnp.where(keep, s * UNIT, FAR))
                blocks.append((held, j))
        top = functools.reduce(
            jnp.maximum, [jnp.max(s, axis=1, keepdims=True) for s in scores]
        )
        total = jnp.zeros_like(top)
        mixed = jnp.zeros((QPK * ROWS, HD), F32)
        for s, (held, j) in zip(scores, blocks):
            weight = jnp.exp2(s - top)
            total = total + jnp.sum(weight, axis=1, keepdims=True)
            mixed = mixed + jnp.dot(weight.astype(BF16), held[layer, j, :, HD:], preferred_element_type=F32)
        shape = (QPK, ROWS)
        return (
            q.reshape(*shape, HD),
            top.reshape(*shape, 1),
            total.reshape(*shape, 1),
            mixed.reshape(*shape, HD),
        )

    upper = lax.broadcasted_iota(jnp.int32, (ROWS, HD), 0) < SEQS

    def by_step(fresh):
        other = jnp.concatenate([fresh[SEQS:], fresh[:SEQS]], axis=0)
        return jnp.where(upper, fresh, other), jnp.where(upper, other, fresh)

    def merge(key, value, part):
        q, top, total, mixed = part
        key_0, key_1 = by_step(key.astype(BF16).astype(F32))
        value_0, value_1 = by_step(value.astype(BF16).astype(F32))
        s_0 = jnp.sum(q * key_0[None], axis=2, keepdims=True) * UNIT
        s_1 = jnp.sum(q * key_1[None], axis=2, keepdims=True) * UNIT
        s_1 = jnp.where(upper[None, :, :1], FAR, s_1)
        peak = jnp.maximum(top, jnp.maximum(s_0, s_1))
        keep = jnp.exp2(top - peak)
        w_0 = jnp.exp2(s_0 - peak)
        w_1 = jnp.exp2(s_1 - peak)
        norm = 1.0 / (total * keep + w_0 + w_1)
        result = (mixed * keep + w_0 * value_0[None] + w_1 * value_1[None]) * norm
        return result.astype(BF16).astype(F32)

    def fold(products):
        products = products.reshape(groups, ROWS, 2 * HD)
        return jnp.concatenate([products[:, :, :HD], products[:, :, HD:]], axis=1).astype(BF16)

    def flatten(features):
        return jnp.concatenate(
            [features[:, :ROWS].reshape(-1, half), features[:, ROWS:].reshape(-1, half)], axis=1
        ).astype(BF16)

    for copy in loads[1:]:
        copy.wait()

    rest = pl.ds(1, groups - 1)
    part_0 = stale(0)
    move(1)
    whole(recv_a.at[rest], recv_sem.at[0]).wait()
    flat = flatten(recv_a[...].astype(F32))
    by_new = jnp.dot(flat, new_0[...], preferred_element_type=F32)
    by_old = jnp.dot(flat, old_0[...], preferred_element_type=F32)
    row_step = lax.rem(lax.broadcasted_iota(jnp.int32, by_new.shape, 0), ROWS) // SEQS
    send_b[...] = fold(jnp.where(row_step >= switch[0], by_new, by_old))
    to_group(send_b, recv_b, 1, -1, True)
    move(2)
    part_1 = stale(1)
    move(3)
    recv_b[0] = send_b[0]

    own = stack_rows(own_v[...])
    whole(recv_b.at[rest], recv_sem.at[1]).wait()
    summed = jnp.sum(recv_b[...].astype(F32), axis=0)
    attended_0 = merge(summed[:ROWS] * scale_0, summed[ROWS:] * scale_0, part_0)
    hidden = [own[:, i * HD : (i + 1) * HD] + attended_0[i] for i in range(QPK)]
    for h in range(2):
        send_c[h] = jnp.concatenate(
            [jnp.concatenate(hidden[4 * h + 2 * r : 4 * h + 2 * r + 2], axis=1) for r in range(2)],
            axis=0,
        ).astype(BF16)

    for step in steps:
        peer = step_from(1, step)
        pltpu.make_async_remote_copy(
            src_ref=send_c.at[lax.rem(core + step[2], 2)],
            dst_ref=recv_c.at[g],
            send_sem=send_sem.at[2],
            recv_sem=recv_sem.at[2],
            device_id=device(peer, t),
            device_id_type=MESH,
        ).start()
    pltpu.make_async_copy(send_c.at[core], recv_c.at[g], recv_sem.at[2]).start()
    for k in range(1, tensors):
        pltpu.make_async_remote_copy(
            src_ref=send_c,
            dst_ref=recv_t.at[t],
            send_sem=send_sem.at[5],
            recv_sem=recv_sem.at[5],
            device_id=device(g, lax.rem(t + k, tensors)),
            device_id_type=MESH,
        ).start()
    pltpu.make_async_copy(send_c, recv_t.at[t], recv_sem.at[5]).start()

    whole(new_1, recv_sem.at[4]).wait()
    whole(recv_c, recv_sem.at[2]).wait()
    flat = flatten(recv_c[...].astype(F32))
    send_d[...] = fold(jnp.dot(flat, new_1[...], preferred_element_type=F32))
    for peer in (1, 0, 3, 2, 13, 12, 5, 4, 15, 14, 7, 6, 9, 8, 11, 10):
        put(send_d.at[peer], recv_d.at[2 * t + core], device(peer, column), 3)

    late.wait()
    whole(recv_t, recv_sem.at[5]).wait()
    parts = [recv_t[i, h].astype(F32) for i in range(tensors) for h in range(2)]
    wide = jnp.concatenate([part[at : at + ROWS] for part in parts for at in (0, ROWS)], axis=1)
    scale_1 = lax.rsqrt(jnp.sum(wide * wide, axis=1, keepdims=True) / width + 1e-05)
    by_old = jnp.dot(wide.astype(BF16), old_1[...], preferred_element_type=F32)
    use_new = lax.broadcasted_iota(jnp.int32, (ROWS, HD), 0) // SEQS >= switch[1]

    whole(recv_d, recv_sem.at[3]).wait()
    summed = jnp.sum(recv_d[...].astype(F32), axis=0)
    key = jnp.where(use_new, summed[:ROWS], by_old[:, :HD]) * scale_1
    value = jnp.where(use_new, summed[ROWS:], by_old[:, HD:]) * scale_1
    attended_1 = merge(key, value, part_1)
    for i in range(QPK):
        rows = (hidden[i] + attended_1[i]).astype(BF16)
        out[0, :, i * HD : (i + 1) * HD] = rows[:SEQS]
        out[1, :, i * HD : (i + 1) * HD] = rows[SEQS:]

    for phase, src in ((0, send_a), (1, send_b), (2, recv_c)):
        whole(src.at[rest], send_sem.at[phase]).wait()
    whole(recv_t.at[pl.ds(1, tensors - 1)], send_sem.at[5]).wait()

    @pl.when(jnp.logical_not(same(there)))
    def _():
        whole(new_1, send_sem.at[4]).wait()

    @pl.when(column != t)
    def _():
        whole(send_d, send_sem.at[3]).wait()

    @pl.when(column == t)
    def _():
        whole(send_d.at[rest], send_sem.at[3]).wait()


def solution(mesh):
    groups, tensors = mesh.shape["group"], mesh.shape["tensor"]

    def per_device(*operands):
        tokens, queries, cache_kv, old_kv, new_kv, switch, lengths = operands
        depth = new_kv.shape[1]
        half = depth // 2
        block = tokens.shape[2] // tensors
        cache_len = cache_kv.shape[2]
        hbm = pl.BlockSpec(memory_space=pltpu.HBM)
        vmem = pltpu.VMEM
        result = pl.pallas_call(
            functools.partial(kernel, groups, tensors),
            out_shape=jax.ShapeDtypeStruct((STEPS, SEQS, block), BF16),
            in_specs=[hbm] * 7,
            out_specs=pl.BlockSpec(memory_space=vmem),
            scratch_shapes=[
                pltpu.SMEM(switch.shape, jnp.int32),
                pltpu.SMEM(lengths.shape, jnp.int32),
                vmem(tokens.shape, BF16),
                vmem((STEPS, SEQS, block), BF16),
                vmem(queries.shape, BF16),
                vmem((LAYERS, 2, cache_len, 2 * HD), BF16),
                vmem((LAYERS, 2, SHORT, 2 * HD), BF16),
                vmem((depth, 2 * HD), BF16),
                vmem(old_kv.shape[1:], BF16),
                vmem((depth, 2 * HD), BF16),
                vmem((depth, 2 * HD), BF16),
                vmem((groups, 2 * ROWS, half), BF16),
                vmem((groups, 2 * ROWS, half), BF16),
                vmem((groups, 2 * ROWS, HD), BF16),
                vmem((groups, 2 * ROWS, HD), BF16),
                vmem((2, 2 * ROWS, half), BF16),
                vmem((groups, 2 * ROWS, half), BF16),
                vmem((tensors, 2, 2 * ROWS, half), BF16),
                vmem((groups, 2 * ROWS, HD), BF16),
                vmem((groups, 2 * ROWS, HD), BF16),
                pltpu.SemaphoreType.DMA((8,)),
                pltpu.SemaphoreType.DMA((LAYERS, 2)),
                pltpu.SemaphoreType.DMA((LAYERS, 2)),
                pltpu.SemaphoreType.DMA((6,)),
                pltpu.SemaphoreType.DMA((6,)),
                pltpu.SemaphoreType.REGULAR,
                pltpu.SemaphoreType.REGULAR,
            ],
            compiler_params=pltpu.CompilerParams(
                collective_id=0, has_side_effects=True, vmem_limit_bytes=40 * 2**20
            ),
        )(*[pltpu.with_memory_space_constraint(operand, pltpu.HBM) for operand in operands])
        return result

    return jax.shard_map(
        per_device,
        mesh=mesh,
        in_specs=(
            P(None, "group", None),
            P(None, None, "group", "tensor"),
            P(None, "group", None, "tensor"),
            P(None, None, "tensor"),
            P(None, "group", "tensor"),
            P(),
            P("group"),
        ),
        out_specs=P(None, "group", "tensor"),
        check_vma=False,
    )
```
